256 devices in a mesh: inst: 16 (over y, x), cell: 16 (over z, core).
Axes of the slice: x: 4, y: 4, z: 8, core: 2. Of those that a mesh axis runs over, the one named last changes fastest.
Arguments:
- state: float32 [16, 4, 512, 2048], P('inst', None, None, 'cell'), may hold values from -1.2 to 3, as said below
- src_inst: int32 [4, 16, 2048], P(None, 'inst', 'cell'), may hold values from 0 to 15, as said below
- src_face: int32 [4, 16, 2048], P(None, 'inst', 'cell'), may hold values from 0 to 2047, as said below
- weights: float32 [4, 16, 2048], P(None, 'inst', 'cell'), may hold values from 0 to 1, as said below
Outputs:
- residual: float32 [16, 4, 512, 2048], P('inst', None, None, 'cell')
- new_state: float32 [16, 4, 512, 2048], P('inst', None, None, 'cell')
The draws below stay inside these ranges and needn't reach their ends.
Inputs may be any that keep to these rules, and one draw needn't show every extreme that they name: `src_inst`: entries of a rotor instance (index below 9) name stator instances, entries of a stator instance name rotor instances; entries 0 and 1 of a face name one instance, entries 2 and 3 the next instance of the same row (cyclically within the row). `src_face`: the sliding interface turns each instance by one pitchwise shift s of its own: for face y of instance i, entries 0 and 2 name face (y + s) mod 2048 and entries 1 and 3 name face (y + s + 1) mod 2048. The 4 weights of a face are non-negative and sum to one. `state`: density within 0.8 to 1.25, momenta within -1.2 to 1.2, energy within 2 to 3.
All inputs are finite; a program needn't handle non-finite values.
Results may differ from the reference program's by a relative error of at most 0.0002.
Values sent between devices are 32-bit elements; how exact they have to be, the bound alone decides.
No kernel may reach another device: no remote copies, remote signals or barrier semaphores. Data moves between devices by JAX's collectives and lax.ppermute only.
A program may use at most 128 MiB of HBM per device.

```python
import jax
import jax.numpy as jnp
import numpy as np
from jax import lax

ROTOR_INST = 9
STATOR_INST = 7
INSTANCES = 16
ENTRIES = 4
NXG = 512
NY = 2048


def draw_state(key, part):
    key = jax.random.fold_in(key, 17)
    keys = jax.random.split(key, 4)
    shape = (INSTANCES, NXG, NY)
    density = jax.random.uniform(keys[0], shape, jnp.float32, 0.8, 1.25)
    momentum_x = jnp.clip(0.4 * jax.random.normal(keys[1], shape, jnp.float32), -1.2, 1.2)
    momentum_y = jnp.clip(0.4 * jax.random.normal(keys[2], shape, jnp.float32), -1.2, 1.2)
    energy = jax.random.uniform(keys[3], shape, jnp.float32, 2.0, 3.0)
    return jnp.stack([density, momentum_x, momentum_y, energy], 1)


def draw_src_inst(key, part):
    key = jax.random.fold_in(key, 11)
    places = jnp.arange(INSTANCES)[:, None]
    is_rotor = places < ROTOR_INST
    others = jnp.where(is_rotor, STATOR_INST, ROTOR_INST)
    offset = jnp.where(is_rotor, ROTOR_INST, 0)
    raw = jax.random.randint(key, (INSTANCES, NY), 0, 1 << 20)
    lower = raw % others
    faces = jnp.arange(NY)[None, :]
    lower = jnp.where(faces == 0, others - 1, lower)
    upper = (lower + 1) % others
    first_src = offset + lower
    second_src = offset + upper
    return jnp.stack([first_src, first_src, second_src, second_src], 0).astype(jnp.int32)


def draw_src_face(key, part):
    key = jax.random.fold_in(key, 23)
    shifts = jax.random.randint(key, (INSTANCES, 1), 0, NY)
    faces = jnp.arange(NY)[None, :]
    lower = (faces + shifts) % NY
    upper = (lower + 1) % NY
    return jnp.stack([lower, upper, lower, upper], 0).astype(jnp.int32)


def draw_weights(key, part):
    key = jax.random.fold_in(key, 31)
    keys = jax.random.split(key, 2)
    time_part = jax.random.uniform(keys[0], (INSTANCES, NY), jnp.float32)
    space_part = jax.random.uniform(keys[1], (INSTANCES, NY), jnp.float32)
    return jnp.stack([(1.0 - time_part) * (1.0 - space_part), (1.0 - time_part) * space_part, time_part * (1.0 - space_part), time_part * space_part], 0)


def setup_inputs(seed: int = 0) -> dict:
    key_list = jax.random.split(jax.random.key(seed), 5)
    state = draw_state(jax.random.fold_in(key_list[4], 71), 0)
    src_inst = draw_src_inst(jax.random.fold_in(key_list[4], 71), 0)
    src_face = draw_src_face(jax.random.fold_in(key_list[4], 71), 0)
    weights = draw_weights(jax.random.fold_in(key_list[4], 71), 0)
    return dict(state=state, src_inst=src_inst, src_face=src_face, weights=weights)


GAMMA_LESS = 0.4
DAMPING_COEF = 0.05
PSEUDO_STEP = 0.2
OMEGA_ROTOR = 0.8
OMEGA_STATOR = 0.6


def spectral_block(count, omega):
    places = np.arange(count)
    distance = places[:, None] - places[None, :]
    off_diag = distance != 0
    safe = np.where(off_diag, distance, 1)
    values = 0.5 * np.power(-1.0, distance) / np.sin(np.pi * safe / count)
    return np.where(off_diag, values, 0.0) * omega


def spectral_table(rotor_count, stator_count):
    total = rotor_count + stator_count
    matrix = np.zeros((total, total))
    matrix[:rotor_count, :rotor_count] = spectral_block(rotor_count, OMEGA_ROTOR)
    matrix[rotor_count:, rotor_count:] = spectral_block(stator_count, OMEGA_STATOR)
    return jnp.asarray(matrix, jnp.float32)


def flux_along(field, axial):
    density = field[:, 0]
    momentum_x = field[:, 1]
    momentum_y = field[:, 2]
    energy = field[:, 3]
    velocity_x = momentum_x / density
    velocity_y = momentum_y / density
    pressure = GAMMA_LESS * (energy - 0.5 * (momentum_x * velocity_x + momentum_y * velocity_y))
    if axial:
        parts = [momentum_x, momentum_x * velocity_x + pressure, momentum_y * velocity_x, (energy + pressure) * velocity_x]
    else:
        parts = [momentum_y, momentum_x * velocity_y, momentum_y * velocity_y + pressure, (energy + pressure) * velocity_y]
    return jnp.stack(parts, 1)


def reference(state, src_inst, src_face, weights):
    count = state.shape[0]
    width = state.shape[3]
    is_rotor = (jnp.arange(count) < ROTOR_INST)[:, None, None]
    export = jnp.where(is_rotor, state[:, :, -1, :], state[:, :, 0, :])
    face_table = jnp.transpose(export, (1, 0, 2)).reshape(4, count * width)
    flat_index = (src_inst * width + src_face).astype(jnp.int32)
    ghost_row = jnp.zeros((4, count, width), jnp.float32)
    for entry in range(ENTRIES):
        ghost_row = ghost_row + weights[entry][None] * face_table[:, flat_index[entry]]
    ghost_row = jnp.transpose(ghost_row, (1, 0, 2))
    left_ghost = jnp.where(is_rotor, state[:, :, 0, :], ghost_row)
    right_ghost = jnp.where(is_rotor, ghost_row, state[:, :, -1, :])
    padded_x = jnp.concatenate([left_ghost[:, :, None], state, right_ghost[:, :, None]], 2)
    padded_y = jnp.concatenate([state[..., -1:], state, state[..., :1]], 3)
    flux_x = flux_along(padded_x, True)
    flux_y = flux_along(padded_y, False)
    convective = 0.5 * (flux_x[:, :, 2:] - flux_x[:, :, :-2]) + 0.5 * (flux_y[..., 2:] - flux_y[..., :-2])
    damping = DAMPING_COEF * (padded_x[:, :, 2:] + padded_x[:, :, :-2] + padded_y[..., 2:] + padded_y[..., :-2] - 4.0 * state)
    couple = spectral_table(ROTOR_INST, STATOR_INST)
    source = jnp.einsum("ij,jcxy->icxy", couple, state, precision=lax.Precision.HIGHEST)
    residual = convective - damping + source
    new_state = state - PSEUDO_STEP * residual
    return residual, new_state
```

```python
import functools

import jax
import jax.numpy as jnp
import numpy as np
from jax import lax
from jax.experimental import pallas as pl
from jax.experimental.pallas import tpu as pltpu
from jax.sharding import PartitionSpec as P

ROTOR_INST = 9
STATOR_INST = 7
INST = ROTOR_INST + STATOR_INST
OMEGA_ROTOR = 0.8
OMEGA_STATOR = 0.6
GAMMA_LESS = 0.4
DAMPING_COEF = 0.05
PSEUDO_STEP = 0.2
LANES = 128
ROWS = 8


def pitch_coefficients(count, omega):
    steps = np.arange(1, (count - 1) // 2 + 1)
    return omega * 0.5 * np.power(-1.0, steps) / np.sin(np.pi * steps / count)


def coupled(values, omega):
    count = len(values)
    coefs = pitch_coefficients(count, omega)
    outs = []
    for i in range(count):
        total = None
        for d, coef in enumerate(coefs, 1):
            term = float(coef) * (values[(i - d) % count] - values[(i + d) % count])
            total = term if total is None else total + term
        outs.append(total)
    return outs


def source_kernel(starts_ref, gathered_ref, faces_ref, out_ref):
    depth = gathered_ref.shape[1]

    def strip(t, carry):
        rows = pl.ds(pl.multiple_of(t * ROWS, ROWS), ROWS)
        values = [gathered_ref[i, rows, :] for i in range(INST)]
        outs = coupled(values[:ROTOR_INST], OMEGA_ROTOR) + coupled(values[ROTOR_INST:], OMEGA_STATOR)
        for i in range(INST):
            out_ref[i, rows, :] = outs[i]
        return carry

    lax.fori_loop(0, depth // ROWS, strip, 0)

    lane = lax.broadcasted_iota(jnp.int32, (ROWS, LANES), 1)
    lower = lax.broadcasted_iota(jnp.int32, (ROWS, LANES), 0) < 4
    slabs = faces_ref.shape[0]
    for i in range(INST):
        start = starts_ref[i]
        slab = lax.rem(start // LANES, slabs)
        offset = lax.rem(start, LANES)
        here = faces_ref[slab]
        after = faces_ref[lax.rem(slab + 1, slabs)]
        turn0 = lax.rem(LANES - offset, LANES)
        turn1 = LANES - 1 - offset
        face0 = jnp.where(lane < LANES - offset, pltpu.roll(here, turn0, 1), pltpu.roll(after, turn0, 1))
        face1 = jnp.where(lane < LANES - 1 - offset, pltpu.roll(here, turn1, 1), pltpu.roll(after, turn1, 1))
        out_ref[i, depth : depth + ROWS, :] = jnp.where(lower, face0, face1)


def fluxes(r, m, n, e):
    inv = 1.0 / r
    a = m * inv
    b = n * inv
    ma = m * a
    mb = m * b
    nb = n * b
    p = GAMMA_LESS * (e - 0.5 * (ma + nb))
    h = e + p
    return (m, ma + p, mb, h * a), (n, mb, nb + p, h * b)


def step_kernel(
    rotor_ref, cur_ref, prev_ref, next_ref, source_ref, window_ref, right_ref, left_ref,
    inst_ref, weight_ref, residual_ref, new_ref, ghost_ref, plus_ref, minus_ref,
):
    block = pl.program_id(0)
    last = pl.num_programs(0) - 1
    size = cur_ref.shape[1]
    rotor = rotor_ref[0] > 0

    @pl.when(block == 0)
    def _():
        total = jnp.zeros((ROWS, LANES), jnp.float32)
        lower = lax.broadcasted_iota(jnp.int32, (ROWS, LANES), 0) < 4

        def spread(ref, first, second):
            return jnp.where(
                lower,
                jnp.broadcast_to(ref[first : first + 1, :], (ROWS, LANES)),
                jnp.broadcast_to(ref[second : second + 1, :], (ROWS, LANES)),
            )

        inst0, inst2 = spread(inst_ref, 0, 1), spread(inst_ref, 2, 3)
        weight0, weight2 = spread(weight_ref, 0, 1), spread(weight_ref, 2, 3)
        for i in range(INST):
            coef = jnp.where(inst0 == i, weight0, 0.0) + jnp.where(inst2 == i, weight2, 0.0)
            total = total + coef * window_ref[i // 4, i % 4]
        ghost_ref[...] = total + pltpu.roll(total, 4, 0)

    def edge(outer, own, at_end, takes_ghost):
        rows = []
        for c in range(4):
            inner = jnp.broadcast_to(own[c], (ROWS, LANES))
            ghost = jnp.broadcast_to(ghost_ref[c : c + 1, :], (ROWS, LANES))
            boundary = jnp.where(takes_ghost, ghost, inner)
            rows.append(jnp.where(at_end, boundary, outer[c]))
        return rows

    before = edge(
        [prev_ref[c] for c in range(4)],
        [cur_ref[c, 0:1, :] for c in range(4)],
        block == 0,
        jnp.logical_not(rotor),
    )
    after = edge(
        [next_ref[c] for c in range(4)],
        [cur_ref[c, size - 1 : size, :] for c in range(4)],
        block == last,
        rotor,
    )
    flux_before, _ = fluxes(*before)
    flux_after, _ = fluxes(*after)
    for c in range(4):
        minus_ref[c, 0:ROWS, :] = 0.5 * flux_before[c] + DAMPING_COEF * before[c]
        plus_ref[c, size + ROWS : size + 2 * ROWS, :] = 0.5 * flux_after[c] - DAMPING_COEF * after[c]

    lane = lax.broadcasted_iota(jnp.int32, (ROWS, LANES), 1)

    def first(t, carry):
        rows = pl.ds(pl.multiple_of(t * ROWS, ROWS), ROWS)
        shifted = pl.ds(pl.multiple_of(t * ROWS + ROWS, ROWS), ROWS)
        u = [cur_ref[c, rows, :] for c in range(4)]
        flux_x, flux_y = fluxes(*u)
        for c in range(4):
            half_x = 0.5 * flux_x[c]
            half_y = 0.5 * flux_y[c]
            damped = DAMPING_COEF * u[c]
            plus_ref[c, shifted, :] = half_x - damped
            minus_ref[c, shifted, :] = half_x + damped
            up = jnp.where(lane == 0, right_ref[c, rows, :], half_y - damped)
            down = jnp.where(lane == LANES - 1, left_ref[c, rows, :], half_y + damped)
            residual_ref[c, rows, :] = (
                pltpu.roll(up, LANES - 1, 1)
                - pltpu.roll(down, 1, 1)
                + (4.0 * DAMPING_COEF) * u[c]
                + source_ref[c, 0, rows, :]
            )
        return carry

    lax.fori_loop(0, size // ROWS, first, 0)

    for t in range(size // ROWS):
        lo = t * ROWS
        for c in range(4):
            out = (
                residual_ref[c, lo : lo + ROWS, :]
                + plus_ref[c, lo + ROWS + 1 : lo + 2 * ROWS + 1, :]
                - minus_ref[c, lo + ROWS - 1 : lo + 2 * ROWS - 1, :]
            )
            residual_ref[c, lo : lo + ROWS, :] = out
            new_ref[c, lo : lo + ROWS, :] = cur_ref[c, lo : lo + ROWS, :] - PSEUDO_STEP * out


def on_device(state, src_inst, src_face, weights):
    cells = state[0]
    axial, width = cells.shape[1], cells.shape[2]
    inst_count = lax.axis_size("inst")
    cell_count = lax.axis_size("cell")
    rotor = lax.axis_index("inst") < ROTOR_INST
    depth = 4 * axial // inst_count

    export = jnp.where(rotor, cells[:, -1, :], cells[:, 0, :])
    faces = lax.all_gather(jnp.concatenate([export, export], 0), "cell", axis=0)
    starts = lax.all_gather(src_face[0, 0, :1], "inst", axis=0, tiled=True)

    head, tail = cells[:, :, 0], cells[:, :, width - 1]
    _, head_flux = fluxes(*head)
    _, tail_flux = fluxes(*tail)
    head = 0.5 * jnp.stack(head_flux) - DAMPING_COEF * head
    tail = 0.5 * jnp.stack(tail_flux) + DAMPING_COEF * tail
    right = lax.ppermute(head, "cell", [((i + 1) % cell_count, i) for i in range(cell_count)])
    left = lax.ppermute(tail, "cell", [(i, (i + 1) % cell_count) for i in range(cell_count)])

    gathered = lax.all_to_all(cells.reshape(inst_count, depth, width), "inst", 0, 0)
    packed = pl.pallas_call(
        source_kernel,
        out_shape=jax.ShapeDtypeStruct((inst_count, depth + ROWS, width), jnp.float32),
        in_specs=[
            pl.BlockSpec(memory_space=pltpu.SMEM),
            pl.BlockSpec(memory_space=pltpu.VMEM),
            pl.BlockSpec(memory_space=pltpu.VMEM),
        ],
        out_specs=pl.BlockSpec(memory_space=pltpu.VMEM),
        compiler_params=pltpu.CompilerParams(vmem_limit_bytes=16 << 20),
        name="source",
    )(starts, gathered, faces)
    packed = lax.all_to_all(packed, "inst", 0, 0).reshape(4, inst_count // 4, depth + ROWS, width)

    blocks = axial // depth
    per = depth // ROWS
    strips = axial // ROWS
    block_spec = pl.BlockSpec((4, depth, width), lambda g: (0, g, 0))
    halo_spec = pl.BlockSpec((4, depth, 1), lambda g: (0, g, 0))
    residual, new_state = pl.pallas_call(
        step_kernel,
        grid=(blocks,),
        out_shape=[jax.ShapeDtypeStruct(cells.shape, jnp.float32)] * 2,
        in_specs=[
            pl.BlockSpec(memory_space=pltpu.SMEM),
            block_spec,
            pl.BlockSpec((4, ROWS, width), lambda g: (0, jnp.maximum(g * per - 1, 0), 0)),
            pl.BlockSpec((4, ROWS, width), lambda g: (0, jnp.minimum(g * per + per, strips - 1), 0)),
            pl.BlockSpec((4, 1, depth, width), lambda g: (0, g, 0, 0)),
            pl.BlockSpec((4, inst_count // 4, ROWS, width), lambda g: (0, 0, per, 0)),
            halo_spec,
            halo_spec,
            pl.BlockSpec((4, width), lambda g: (0, 0)),
            pl.BlockSpec((4, width), lambda g: (0, 0)),
        ],
        out_specs=[block_spec, block_spec],
        scratch_shapes=[
            pltpu.VMEM((ROWS, width), jnp.float32),
            pltpu.VMEM((4, depth + 2 * ROWS, width), jnp.float32),
            pltpu.VMEM((4, depth + 2 * ROWS, width), jnp.float32),
        ],
        compiler_params=pltpu.CompilerParams(vmem_limit_bytes=16 << 20),
        name="step",
    )(
        rotor.astype(jnp.int32)[None],
        cells, cells, cells, packed, packed, right[:, :, None], left[:, :, None],
        src_inst[:, 0, :], weights[:, 0, :],
    )
    return residual[None], new_state[None]


def solution(mesh):
    return jax.shard_map(
        on_device,
        mesh=mesh,
        in_specs=(
            P("inst", None, None, "cell"),
            P(None, "inst", "cell"),
            P(None, "inst", "cell"),
            P(None, "inst", "cell"),
        ),
        out_specs=(P("inst", None, None, "cell"), P("inst", None, None, "cell")),
        check_vma=False,
    )
```

```python
import jax
import jax.numpy as jnp
import numpy as np
from jax import lax
from jax.experimental import pallas as pl
from jax.experimental.pallas import tpu as pltpu
from jax.sharding import PartitionSpec as P

ROTOR_INST = 9
STATOR_INST = 7
INST = ROTOR_INST + STATOR_INST
OMEGA_ROTOR = 0.8
OMEGA_STATOR = 0.6
GAMMA_LESS = 0.4
DAMPING_COEF = 0.05
PSEUDO_STEP = 0.2
LANES = 128
ROWS = 8


def pitch_coefficients(count, omega):
    steps = np.arange(1, (count - 1) // 2 + 1)
    return omega * 0.5 * np.power(-1.0, steps) / np.sin(np.pi * steps / count)


def coupled(values, omega):
    count = len(values)
    coefs = pitch_coefficients(count, omega)
    outs = []
    for i in range(count):
        total = None
        for d, coef in enumerate(coefs, 1):
            term = float(coef) * (values[(i - d) % count] - values[(i + d) % count])
            total = term if total is None else total + term
        outs.append(total)
    return outs


def send_kernel(cells_ref, face_ref, out_ref, want_ref, sems):
    depth = out_ref.shape[1] - ROWS
    asked = pltpu.make_async_copy(face_ref, want_ref, sems.at[0])
    asked.start()
    chunks = pltpu.make_async_copy(cells_ref, out_ref.at[:, pl.ds(0, depth), :], sems.at[1])
    chunks.start()
    asked.wait()
    lower = lax.broadcasted_iota(jnp.int32, (ROWS, LANES), 0) < 4
    want = jnp.where(
        lower,
        jnp.broadcast_to(want_ref[0], (ROWS, LANES)),
        jnp.broadcast_to(want_ref[1], (ROWS, LANES)),
    ).astype(jnp.float32)
    for j in range(out_ref.shape[0]):
        out_ref[j, depth : depth + ROWS, :] = want
    chunks.wait()


def source_kernel(gathered_ref, faces_ref, out_ref):
    depth = gathered_ref.shape[1] - ROWS
    slab = lax.axis_index("cell")

    def strip(t, carry):
        rows = pl.ds(pl.multiple_of(t * ROWS, ROWS), ROWS)
        values = [gathered_ref[i, rows, :] for i in range(INST)]
        outs = coupled(values[:ROTOR_INST], OMEGA_ROTOR) + coupled(values[ROTOR_INST:], OMEGA_STATOR)
        for i in range(INST):
            out_ref[i, rows, :] = outs[i]
        return carry

    lax.fori_loop(0, depth // ROWS, strip, 0, unroll=2)

    slabs = faces_ref.shape[0] // ROWS
    wants = [gathered_ref[i, depth : depth + ROWS, :].astype(jnp.int32) for i in range(INST)]
    firsts = [(want[0, 0] >> 7) & (slabs - 1) for want in wants]
    windows = []
    for want, first in zip(wants, firsts):
        ahead = (first - slab) & (slabs - 1)
        here = faces_ref[pl.ds(pl.multiple_of(ahead * ROWS, ROWS), ROWS), :]
        ahead = (ahead + 1) & (slabs - 1)
        after = faces_ref[pl.ds(pl.multiple_of(ahead * ROWS, ROWS), ROWS), :]
        place = want & (LANES - 1)
        here = jnp.take_along_axis(here, place, axis=1, mode="promise_in_bounds")
        after = jnp.take_along_axis(after, place, axis=1, mode="promise_in_bounds")
        windows.append(jnp.where((want >> 7) == first, here, after))
    for i in range(INST):
        out_ref[i, depth : depth + ROWS, :] = windows[i]


def fluxes(r, m, n, e):
    inv = 1.0 / r
    a = m * inv
    b = n * inv
    ma = m * a
    mb = m * b
    nb = n * b
    p = GAMMA_LESS * (e - 0.5 * (ma + nb))
    h = e + p
    return (m, ma + p, mb, h * a), (n, mb, nb + p, h * b)


def partial_kernel(
    cur_ref, prev_ref, next_ref, right_ref, left_ref, out_ref, plus_ref, minus_ref
):
    block = pl.program_id(0)
    last = pl.num_programs(0) - 1
    size = cur_ref.shape[1]
    rotor = lax.axis_index("inst") < ROTOR_INST

    def edge(outer, own, at_end):
        return [jnp.where(at_end, jnp.broadcast_to(own[c], (ROWS, LANES)), outer[c]) for c in range(4)]

    before = edge([prev_ref[c] for c in range(4)], [cur_ref[c, 0:1, :] for c in range(4)], block == 0)
    after = edge(
        [next_ref[c] for c in range(4)], [cur_ref[c, size - 1 : size, :] for c in range(4)], block == last
    )
    keep_before = jnp.where(jnp.logical_or(block > 0, rotor), 1.0, 0.0)
    keep_after = jnp.where(jnp.logical_and(block == last, rotor), 0.0, 1.0)
    flux_before, _ = fluxes(*before)
    flux_after, _ = fluxes(*after)
    for c in range(4):
        minus_ref[c, 0:ROWS, :] = keep_before * (0.5 * flux_before[c] + DAMPING_COEF * before[c])
        plus_ref[c, size + ROWS : size + 2 * ROWS, :] = keep_after * (
            0.5 * flux_after[c] - DAMPING_COEF * after[c]
        )

    lane = lax.broadcasted_iota(jnp.int32, (ROWS, LANES), 1)

    def first(t, carry):
        rows = pl.ds(pl.multiple_of(t * ROWS, ROWS), ROWS)
        shifted = pl.ds(pl.multiple_of(t * ROWS + ROWS, ROWS), ROWS)
        u = [cur_ref[c, rows, :] for c in range(4)]
        flux_x, flux_y = fluxes(*u)
        for c in range(4):
            half_x = 0.5 * flux_x[c]
            half_y = 0.5 * flux_y[c]
            damped = DAMPING_COEF * u[c]
            plus_ref[c, shifted, :] = half_x - damped
            minus_ref[c, shifted, :] = half_x + damped
            up = jnp.where(lane == 0, right_ref[c, rows, :], half_y - damped)
            down = jnp.where(lane == LANES - 1, left_ref[c, rows, :], half_y + damped)
            out_ref[c, rows, :] = (
                pltpu.roll(up, LANES - 1, 1) - pltpu.roll(down, 1, 1) + (4.0 * DAMPING_COEF) * u[c]
            )
        return carry

    lax.fori_loop(0, size // ROWS, first, 0, unroll=4)

    for t in range(size // ROWS):
        lo = t * ROWS
        for c in range(4):
            out_ref[c, lo : lo + ROWS, :] = (
                out_ref[c, lo : lo + ROWS, :]
                + plus_ref[c, lo + ROWS + 1 : lo + 2 * ROWS + 1, :]
                - minus_ref[c, lo + ROWS - 1 : lo + 2 * ROWS - 1, :]
            )


def finish_kernel(
    packed_ref, partial_ref, cells_ref, inst_ref, weight_ref, residual_ref, new_ref, res_ref, next_ref, sems
):
    rotor = lax.axis_index("inst") < ROTOR_INST
    axial = cells_ref.shape[1]
    depth = packed_ref.shape[1] - ROWS
    per = axial // depth
    row = lax.broadcasted_iota(jnp.int32, (ROWS, LANES), 0)
    lower = row < 4

    def spread(ref, first, second):
        return jnp.where(
            lower,
            jnp.broadcast_to(ref[first : first + 1, :], (ROWS, LANES)),
            jnp.broadcast_to(ref[second : second + 1, :], (ROWS, LANES)),
        )

    inst0, inst2 = spread(inst_ref, 0, 1), spread(inst_ref, 2, 3)
    weight0, weight2 = spread(weight_ref, 0, 1), spread(weight_ref, 2, 3)
    total = jnp.zeros((ROWS, LANES), jnp.float32)
    for i in range(INST):
        coef = jnp.where(inst0 == i, weight0, 0.0) + jnp.where(inst2 == i, weight2, 0.0)
        total = total + coef * packed_ref[i, depth : depth + ROWS, :]
    ghost = total + pltpu.roll(total, 4, 0)
    ghost = [jnp.broadcast_to(ghost[c : c + 1, :], (ROWS, LANES)) for c in range(4)]
    flux_x, _ = fluxes(*ghost)
    head = jnp.logical_and(row == 0, jnp.logical_not(rotor))
    tail = jnp.logical_and(row == ROWS - 1, rotor)
    copies = []
    for c in range(4):
        half, damped = 0.5 * flux_x[c], DAMPING_COEF * ghost[c]
        at_head = jnp.where(head, -half - damped, 0.0)
        at_tail = jnp.where(tail, half - damped, 0.0)
        for j in range(per):

            def strip(t, carry, c=c, j=j):
                rows = pl.ds(pl.multiple_of(j * depth + t * ROWS, ROWS), ROWS)
                mine = pl.ds(pl.multiple_of(t * ROWS, ROWS), ROWS)
                out = partial_ref[c, rows, :] + packed_ref[c * per + j, mine, :]
                res_ref[c, rows, :] = out
                next_ref[c, rows, :] = cells_ref[c, rows, :] - PSEUDO_STEP * out
                return carry

            lax.fori_loop(0, depth // ROWS, strip, 0, unroll=True)
        for first, extra in ((0, at_head), (axial - ROWS, at_tail)):
            out = res_ref[c, first : first + ROWS, :] + extra
            res_ref[c, first : first + ROWS, :] = out
            next_ref[c, first : first + ROWS, :] = cells_ref[c, first : first + ROWS, :] - PSEUDO_STEP * out
        for k, (src, dst) in enumerate(((res_ref, residual_ref), (next_ref, new_ref))):
            copy = pltpu.make_async_copy(src.at[c], dst.at[c], sems.at[2 * c + k])
            copy.start()
            copies.append(copy)
    for copy in copies:
        copy.wait()


def collected(block, axis):
    count = lax.axis_size(axis)
    step = 1
    while step < count:
        pairs = [((i + step) % count, i) for i in range(count)]
        block = jnp.concatenate([block, lax.ppermute(block, axis, pairs)], 0)
        step *= 2
    return block


def on_device(state, src_inst, src_face, weights):
    cells = state[0]
    axial, width = cells.shape[1], cells.shape[2]
    inst_count = lax.axis_size("inst")
    cell_count = lax.axis_size("cell")
    rotor = lax.axis_index("inst") < ROTOR_INST
    depth = 4 * axial // inst_count

    vmem = pl.BlockSpec(memory_space=pltpu.VMEM)
    anywhere = pl.BlockSpec(memory_space=pl.ANY)
    sent = pl.pallas_call(
        send_kernel,
        out_shape=pltpu.VMEM((inst_count, depth + ROWS, width), jnp.float32),
        in_specs=[anywhere, anywhere],
        out_specs=vmem,
        scratch_shapes=[pltpu.VMEM(src_face.shape, jnp.int32), pltpu.SemaphoreType.DMA((2,))],
        compiler_params=pltpu.CompilerParams(vmem_limit_bytes=16 << 20),
        name="send",
    )(cells.reshape(inst_count, depth, width), src_face)
    gathered = lax.all_to_all(sent, "inst", 0, 0)
    export = jnp.where(rotor, cells[:, -1, :], cells[:, 0, :])
    faces = collected(jnp.concatenate([export, export], 0), "cell")
    packed = pl.pallas_call(
        source_kernel,
        out_shape=pltpu.VMEM((inst_count, depth + ROWS, width), jnp.float32),
        in_specs=[vmem, vmem],
        out_specs=vmem,
        compiler_params=pltpu.CompilerParams(vmem_limit_bytes=16 << 20),
        name="source",
    )(gathered, faces)
    cells, packed = lax.optimization_barrier((cells, packed))
    packed = lax.all_to_all(packed, "inst", 0, 0)

    head, tail = cells[:, :, 0], cells[:, :, width - 1]
    _, head_flux = fluxes(*head)
    _, tail_flux = fluxes(*tail)
    head = 0.5 * jnp.stack(head_flux) - DAMPING_COEF * head
    tail = 0.5 * jnp.stack(tail_flux) + DAMPING_COEF * tail
    right = lax.ppermute(head, "cell", [((i + 1) % cell_count, i) for i in range(cell_count)])
    left = lax.ppermute(tail, "cell", [(i, (i + 1) % cell_count) for i in range(cell_count)])

    blocks = axial // depth
    per = depth // ROWS
    strips = axial // ROWS
    block_spec = pl.BlockSpec((4, depth, width), lambda g: (0, g, 0))
    halo_spec = pl.BlockSpec((4, depth, 1), lambda g: (0, g, 0))
    partial = pl.pallas_call(
        partial_kernel,
        grid=(blocks,),
        out_shape=pltpu.VMEM(cells.shape, jnp.float32),
        in_specs=[
            block_spec,
            pl.BlockSpec((4, ROWS, width), lambda g: (0, jnp.maximum(g * per - 1, 0), 0)),
            pl.BlockSpec((4, ROWS, width), lambda g: (0, jnp.minimum(g * per + per, strips - 1), 0)),
            halo_spec,
            halo_spec,
        ],
        out_specs=block_spec,
        scratch_shapes=[
            pltpu.VMEM((4, depth + 2 * ROWS, width), jnp.float32),
            pltpu.VMEM((4, depth + 2 * ROWS, width), jnp.float32),
        ],
        compiler_params=pltpu.CompilerParams(vmem_limit_bytes=16 << 20),
        cost_estimate=pl.CostEstimate(flops=100 * cells.size, bytes_accessed=16 * cells.size, transcendentals=0),
        name="partial",
    )(cells, cells, cells, right[:, :, None], left[:, :, None])
    residual, new_state = pl.pallas_call(
        finish_kernel,
        out_shape=[jax.ShapeDtypeStruct(cells.shape, jnp.float32)] * 2,
        in_specs=[vmem] * 5,
        out_specs=[anywhere, anywhere],
        scratch_shapes=[
            pltpu.VMEM(cells.shape, jnp.float32),
            pltpu.VMEM(cells.shape, jnp.float32),
            pltpu.SemaphoreType.DMA((8,)),
        ],
        compiler_params=pltpu.CompilerParams(vmem_limit_bytes=16 << 20),
        name="finish",
    )(packed, partial, cells, src_inst[:, 0, :], weights[:, 0, :])
    return residual[None], new_state[None]


def solution(mesh):
    return jax.shard_map(
        on_device,
        mesh=mesh,
        in_specs=(
            P("inst", None, None, "cell"),
            P(None, "inst", "cell"),
            P(None, "inst", "cell"),
            P(None, "inst", "cell"),
        ),
        out_specs=(P("inst", None, None, "cell"), P("inst", None, None, "cell")),
        check_vma=False,
    )
```

```python
import jax
import jax.numpy as jnp
import numpy as np
from jax import lax
from jax.experimental import pallas as pl
from jax.experimental.pallas import tpu as pltpu
from jax.sharding import PartitionSpec as P

ROTOR_INST = 9
STATOR_INST = 7
INST = ROTOR_INST + STATOR_INST
OMEGA_ROTOR = 0.8
OMEGA_STATOR = 0.6
GAMMA_LESS = 0.4
DAMPING_COEF = 0.05
PSEUDO_STEP = 0.2
LANES = 128
ROWS = 8
PIECES = 4


def pitch_coefficients(count, omega):
    steps = np.arange(1, (count - 1) // 2 + 1)
    return omega * 0.5 * np.power(-1.0, steps) / np.sin(np.pi * steps / count)


def coupled(values, omega):
    count = len(values)
    coefs = pitch_coefficients(count, omega)
    outs = []
    for i in range(count):
        total = None
        for d, coef in enumerate(coefs, 1):
            term = float(coef) * (values[(i - d) % count] - values[(i + d) % count])
            total = term if total is None else total + term
        outs.append(total)
    return outs


def send_kernel(cells_ref, face_ref, out_ref, held_ref, want_ref, sems):
    count, depth = out_ref.shape[0], out_ref.shape[1] - ROWS
    group = count // PIECES
    asked = pltpu.make_async_copy(face_ref, want_ref, sems.at[0])
    asked.start()
    arrivals = []
    for p in range(PIECES):
        part = pl.ds(p * group, group)
        copy = pltpu.make_async_copy(cells_ref.at[part], held_ref.at[part, pl.ds(0, depth), :], sems.at[1 + p])
        copy.start()
        arrivals.append(copy)
    asked.wait()
    lower = lax.broadcasted_iota(jnp.int32, (ROWS, LANES), 0) < 4
    want = jnp.where(
        lower,
        jnp.broadcast_to(want_ref[0], (ROWS, LANES)),
        jnp.broadcast_to(want_ref[1], (ROWS, LANES)),
    ).astype(jnp.float32)
    for j in range(count):
        held_ref[j, depth : depth + ROWS, :] = want
    leaving = []
    for p in range(PIECES):
        part = pl.ds(p * group, group)
        arrivals[p].wait()
        copy = pltpu.make_async_copy(held_ref.at[part], out_ref.at[part], sems.at[1 + PIECES + p])
        copy.start()
        leaving.append(copy)
    for copy in leaving:
        copy.wait()


def source_kernel(gathered_ref, faces_ref, out_ref, held_ref, sems):
    depth = gathered_ref.shape[1] - ROWS
    slab = lax.axis_index("cell")
    slabs = faces_ref.shape[0] // ROWS
    span = depth // PIECES
    leaving = []

    def leave(k, first, size):
        part = pl.ds(first, size)
        copy = pltpu.make_async_copy(held_ref.at[:, part, :], out_ref.at[:, part, :], sems.at[k])
        copy.start()
        leaving.append(copy)

    def tile(ahead):
        place = (ahead & 3) * (slabs // 4) + (ahead >> 2)
        return faces_ref[pl.ds(pl.multiple_of(place * ROWS, ROWS), ROWS), :]

    wants = [gathered_ref[i, depth : depth + ROWS, :].astype(jnp.int32) for i in range(INST)]
    firsts = [want[0, 0] >> 7 for want in wants]

    for p in range(PIECES):
        for t in range(p * span, (p + 1) * span, ROWS):
            values = [gathered_ref[i, t : t + ROWS, :] for i in range(INST)]
            outs = coupled(values[:ROTOR_INST], OMEGA_ROTOR) + coupled(values[ROTOR_INST:], OMEGA_STATOR)
            for i in range(INST):
                held_ref[i, t : t + ROWS, :] = outs[i]
        if p < PIECES - 1:
            leave(p, p * span, span)
    for i, (want, first) in enumerate(zip(wants, firsts)):
        ahead = (first - slab) & (slabs - 1)
        place = want & (LANES - 1)
        here = jnp.take_along_axis(tile(ahead), place, axis=1, mode="promise_in_bounds")
        after = jnp.take_along_axis(tile((ahead + 1) & (slabs - 1)), place, axis=1, mode="promise_in_bounds")
        held_ref[i, depth : depth + ROWS, :] = jnp.where((want >> 7) == first, here, after)
    leave(PIECES - 1, depth - span, span + ROWS)
    for copy in leaving:
        copy.wait()


def fluxes(r, m, n, e):
    inv = 1.0 / r
    a = m * inv
    b = n * inv
    ma = m * a
    mb = m * b
    nb = n * b
    p = GAMMA_LESS * (e - 0.5 * (ma + nb))
    h = e + p
    return (m, ma + p, mb, h * a), (n, mb, nb + p, h * b)


def edge_kernel(cells_ref, export_ref, head_ref, tail_ref):
    axial = cells_ref.shape[1]
    rotor = lax.axis_index("inst") < ROTOR_INST
    for c in range(4):
        row = jnp.where(rotor, cells_ref[c, axial - 1 : axial, :], cells_ref[c, 0:1, :])
        export_ref[c : c + 1, :] = row
        export_ref[4 + c : 5 + c, :] = row
    lane = lax.broadcasted_iota(jnp.int32, (LANES, LANES), 1)
    for first in range(0, axial, LANES):
        span = pl.ds(first, LANES)
        sides = jnp.zeros((LANES, LANES), jnp.float32)
        for c in range(4):
            u = cells_ref[c, span, :]
            sides = jnp.where(lane == c, pltpu.roll(u, c, 1) if c else u, sides)
            sides = jnp.where(lane == 4 + c, pltpu.roll(u, 5 + c, 1), sides)
        sides = sides.T
        for ref, at, sign in ((head_ref, 0, -1.0), (tail_ref, 4, 1.0)):
            u = [sides[at + c : at + c + 1, :] for c in range(4)]
            _, flux_y = fluxes(*u)
            for c in range(4):
                ref[c : c + 1, span] = 0.5 * flux_y[c] + sign * DAMPING_COEF * u[c]


def partial_kernel(
    cur_ref, prev_ref, next_ref, right_ref, left_ref, out_ref, plus_ref, minus_ref, side_ref
):
    block = pl.program_id(0)
    last = pl.num_programs(0) - 1
    size = cur_ref.shape[1]
    rotor = lax.axis_index("inst") < ROTOR_INST

    def edge(outer, own, at_end):
        return [jnp.where(at_end, jnp.broadcast_to(own[c], (ROWS, LANES)), outer[c]) for c in range(4)]

    before = edge([prev_ref[c] for c in range(4)], [cur_ref[c, 0:1, :] for c in range(4)], block == 0)
    after = edge(
        [next_ref[c] for c in range(4)], [cur_ref[c, size - 1 : size, :] for c in range(4)], block == last
    )
    keep_before = jnp.where(jnp.logical_or(block > 0, rotor), 1.0, 0.0)
    keep_after = jnp.where(jnp.logical_and(block == last, rotor), 0.0, 1.0)
    flux_before, _ = fluxes(*before)
    flux_after, _ = fluxes(*after)
    for c in range(4):
        minus_ref[c, 0:ROWS, :] = keep_before * (0.5 * flux_before[c] + DAMPING_COEF * before[c])
        plus_ref[c, size + ROWS : size + 2 * ROWS, :] = keep_after * (
            0.5 * flux_after[c] - DAMPING_COEF * after[c]
        )

    lane = lax.broadcasted_iota(jnp.int32, (ROWS, LANES), 1)
    sides = jnp.concatenate([right_ref[...], left_ref[...], jnp.zeros((LANES - 8, LANES), jnp.float32)], 0)
    side_ref[...] = sides.T

    def first(t, carry):
        rows = pl.ds(pl.multiple_of(t * ROWS, ROWS), ROWS)
        shifted = pl.ds(pl.multiple_of(t * ROWS + ROWS, ROWS), ROWS)
        u = [cur_ref[c, rows, :] for c in range(4)]
        flux_x, flux_y = fluxes(*u)
        side = side_ref[rows, :]
        for c in range(4):
            half_x = 0.5 * flux_x[c]
            half_y = 0.5 * flux_y[c]
            damped = DAMPING_COEF * u[c]
            plus_ref[c, shifted, :] = half_x - damped
            minus_ref[c, shifted, :] = half_x + damped
            up = jnp.where(lane == 0, jnp.broadcast_to(side[:, c : c + 1], (ROWS, LANES)), half_y - damped)
            down = jnp.where(lane == LANES - 1, jnp.broadcast_to(side[:, 4 + c : 5 + c], (ROWS, LANES)), half_y + damped)
            out_ref[c, rows, :] = (
                pltpu.roll(up, LANES - 1, 1) - pltpu.roll(down, 1, 1) + (4.0 * DAMPING_COEF) * u[c]
            )
        return carry

    lax.fori_loop(0, size // ROWS, first, 0, unroll=4)

    for t in range(size // ROWS):
        lo = t * ROWS
        for c in range(4):
            out_ref[c, lo : lo + ROWS, :] = (
                out_ref[c, lo : lo + ROWS, :]
                + plus_ref[c, lo + ROWS + 1 : lo + 2 * ROWS + 1, :]
                - minus_ref[c, lo + ROWS - 1 : lo + 2 * ROWS - 1, :]
            )


def finish_kernel(
    packed_ref, partial_ref, cells_ref, inst_ref, weight_ref, residual_ref, new_ref, res_ref, next_ref, sems
):
    rotor = lax.axis_index("inst") < ROTOR_INST
    axial = cells_ref.shape[1]
    depth = packed_ref.shape[1] - ROWS
    per = axial // depth
    row = lax.broadcasted_iota(jnp.int32, (ROWS, LANES), 0)
    lower = row < 4

    def spread(ref, first, second):
        return jnp.where(
            lower,
            jnp.broadcast_to(ref[first : first + 1, :], (ROWS, LANES)),
            jnp.broadcast_to(ref[second : second + 1, :], (ROWS, LANES)),
        )

    inst0, inst2 = spread(inst_ref, 0, 1), spread(inst_ref, 2, 3)
    weight0, weight2 = spread(weight_ref, 0, 1), spread(weight_ref, 2, 3)
    total = jnp.zeros((ROWS, LANES), jnp.float32)
    for i in range(INST):
        coef = jnp.where(inst0 == i, weight0, 0.0) + jnp.where(inst2 == i, weight2, 0.0)
        total = total + coef * packed_ref[i, depth : depth + ROWS, :]
    ghost = total + pltpu.roll(total, 4, 0)
    ghost = [jnp.broadcast_to(ghost[c : c + 1, :], (ROWS, LANES)) for c in range(4)]
    flux_x, _ = fluxes(*ghost)
    head = jnp.logical_and(row == 0, jnp.logical_not(rotor))
    tail = jnp.logical_and(row == ROWS - 1, rotor)
    copies = []
    for c in range(4):
        half, damped = 0.5 * flux_x[c], DAMPING_COEF * ghost[c]
        at_head = jnp.where(head, -half - damped, 0.0)
        at_tail = jnp.where(tail, half - damped, 0.0)
        for j in range(per):

            def strip(t, carry, c=c, j=j):
                rows = pl.ds(pl.multiple_of(j * depth + t * ROWS, ROWS), ROWS)
                mine = pl.ds(pl.multiple_of(t * ROWS, ROWS), ROWS)
                out = partial_ref[c, rows, :] + packed_ref[c * per + j, mine, :]
                res_ref[c, rows, :] = out
                next_ref[c, rows, :] = cells_ref[c, rows, :] - PSEUDO_STEP * out
                return carry

            lax.fori_loop(0, depth // ROWS, strip, 0, unroll=True)
        for first, extra in ((0, at_head), (axial - ROWS, at_tail)):
            out = res_ref[c, first : first + ROWS, :] + extra
            res_ref[c, first : first + ROWS, :] = out
            next_ref[c, first : first + ROWS, :] = cells_ref[c, first : first + ROWS, :] - PSEUDO_STEP * out
        for k, (src, dst) in enumerate(((res_ref, residual_ref), (next_ref, new_ref))):
            copy = pltpu.make_async_copy(src.at[c], dst.at[c], sems.at[2 * c + k])
            copy.start()
            copies.append(copy)
    for copy in copies:
        copy.wait()


def collected(block, axis):
    count = lax.axis_size(axis)
    for step in (count // 4, 1):
        blocks = [block]
        for k in range(1, 4):
            pairs = [((i + k * step) % count, i) for i in range(count)]
            blocks.append(lax.ppermute(block, axis, pairs))
        block = jnp.concatenate(blocks, 0)
    return block


def on_device(state, src_inst, src_face, weights):
    cells = state[0]
    axial, width = cells.shape[1], cells.shape[2]
    inst_count = lax.axis_size("inst")
    cell_count = lax.axis_size("cell")
    depth = 4 * axial // inst_count

    vmem = pl.BlockSpec(memory_space=pltpu.VMEM)
    anywhere = pl.BlockSpec(memory_space=pl.ANY)
    sent = pl.pallas_call(
        send_kernel,
        out_shape=jax.ShapeDtypeStruct((inst_count, depth + ROWS, width), jnp.float32),
        in_specs=[anywhere, anywhere],
        out_specs=anywhere,
        scratch_shapes=[
            pltpu.VMEM((inst_count, depth + ROWS, width), jnp.float32),
            pltpu.VMEM(src_face.shape, jnp.int32),
            pltpu.SemaphoreType.DMA((1 + 2 * PIECES,)),
        ],
        compiler_params=pltpu.CompilerParams(vmem_limit_bytes=60 << 20),
        name="send",
    )(cells.reshape(inst_count, depth, width), src_face)
    sent, cells = lax.optimization_barrier((sent, cells))
    export, head, tail = pl.pallas_call(
        edge_kernel,
        out_shape=[
            jax.ShapeDtypeStruct((ROWS, width), jnp.float32),
            jax.ShapeDtypeStruct((4, axial), jnp.float32),
            jax.ShapeDtypeStruct((4, axial), jnp.float32),
        ],
        in_specs=[vmem],
        out_specs=[vmem] * 3,
        compiler_params=pltpu.CompilerParams(vmem_limit_bytes=16 << 20),
        cost_estimate=pl.CostEstimate(flops=0, bytes_accessed=32 << 20, transcendentals=0),
        name="edges",
    )(cells)
    gathered = lax.all_to_all(sent, "inst", 0, 0)
    faces = collected(export, "cell")
    packed = pl.pallas_call(
        source_kernel,
        out_shape=jax.ShapeDtypeStruct((inst_count, depth + ROWS, width), jnp.float32),
        in_specs=[vmem, vmem],
        out_specs=anywhere,
        scratch_shapes=[
            pltpu.VMEM((inst_count, depth + ROWS, width), jnp.float32),
            pltpu.SemaphoreType.DMA((PIECES,)),
        ],
        compiler_params=pltpu.CompilerParams(vmem_limit_bytes=16 << 20),
        name="source",
    )(gathered, faces)
    head, tail, packed = lax.optimization_barrier((head, tail, packed))
    packed = lax.all_to_all(packed, "inst", 0, 0)

    right = lax.ppermute(head, "cell", [((i + 1) % cell_count, i) for i in range(cell_count)])
    left = lax.ppermute(tail, "cell", [(i, (i + 1) % cell_count) for i in range(cell_count)])

    blocks = axial // depth
    per = depth // ROWS
    strips = axial // ROWS
    block_spec = pl.BlockSpec((4, depth, width), lambda g: (0, g, 0))
    halo_spec = pl.BlockSpec((4, depth), lambda g: (0, g))
    partial = pl.pallas_call(
        partial_kernel,
        grid=(blocks,),
        out_shape=pltpu.VMEM(cells.shape, jnp.float32),
        in_specs=[
            block_spec,
            pl.BlockSpec((4, ROWS, width), lambda g: (0, jnp.maximum(g * per - 1, 0), 0)),
            pl.BlockSpec((4, ROWS, width), lambda g: (0, jnp.minimum(g * per + per, strips - 1), 0)),
            halo_spec,
            halo_spec,
        ],
        out_specs=block_spec,
        scratch_shapes=[
            pltpu.VMEM((4, depth + 2 * ROWS, width), jnp.float32),
            pltpu.VMEM((4, depth + 2 * ROWS, width), jnp.float32),
            pltpu.VMEM((depth, width), jnp.float32),
        ],
        compiler_params=pltpu.CompilerParams(vmem_limit_bytes=16 << 20),
        cost_estimate=pl.CostEstimate(flops=100 * cells.size, bytes_accessed=16 * cells.size, transcendentals=0),
        name="partial",
    )(cells, cells, cells, right, left)
    residual, new_state = pl.pallas_call(
        finish_kernel,
        out_shape=[jax.ShapeDtypeStruct(cells.shape, jnp.float32)] * 2,
        in_specs=[vmem] * 5,
        out_specs=[anywhere, anywhere],
        scratch_shapes=[
            pltpu.VMEM(cells.shape, jnp.float32),
            pltpu.VMEM(cells.shape, jnp.float32),
            pltpu.SemaphoreType.DMA((8,)),
        ],
        compiler_params=pltpu.CompilerParams(vmem_limit_bytes=16 << 20),
        name="finish",
    )(packed, partial, cells, src_inst[:, 0, :], weights[:, 0, :])
    return residual[None], new_state[None]


def solution(mesh):
    return jax.shard_map(
        on_device,
        mesh=mesh,
        in_specs=(
            P("inst", None, None, "cell"),
            P(None, "inst", "cell"),
            P(None, "inst", "cell"),
            P(None, "inst", "cell"),
        ),
        out_specs=(P("inst", None, None, "cell"), P("inst", None, None, "cell")),
        check_vma=False,
    )
```

```python
import jax
import jax.numpy as jnp
import numpy as np
from jax import lax
from jax.experimental import pallas as pl
from jax.experimental.pallas import tpu as pltpu
from jax.sharding import PartitionSpec as P

ROTOR_INST = 9
STATOR_INST = 7
INST = ROTOR_INST + STATOR_INST
OMEGA_ROTOR = 0.8
OMEGA_STATOR = 0.6
GAMMA_LESS = 0.4
DAMPING_COEF = 0.05
PSEUDO_STEP = 0.2
LANES = 128
ROWS = 8
PIECES = 4
ORDER = (8, 12, 3, 4, 6, 15, 10, 14, 13, 1, 9, 2, 5, 7, 0, 11)


def pitch_coefficients(count, omega):
    steps = np.arange(1, (count - 1) // 2 + 1)
    return omega * 0.5 * np.power(-1.0, steps) / np.sin(np.pi * steps / count)


def coupled(values, omega):
    count = len(values)
    coefs = pitch_coefficients(count, omega)
    outs = []
    for i in range(count):
        total = None
        for d, coef in enumerate(coefs, 1):
            term = float(coef) * (values[(i - d) % count] - values[(i + d) % count])
            total = term if total is None else total + term
        outs.append(total)
    return outs


def send_kernel(cells_ref, face_ref, out_ref, held_ref, want_ref, sems):
    count, depth = out_ref.shape[0], out_ref.shape[1] - ROWS
    group = count // PIECES
    asked = pltpu.make_async_copy(face_ref, want_ref, sems.at[0])
    asked.start()
    arrivals = []
    for p in range(PIECES):
        part = pl.ds(p * group, group)
        copy = pltpu.make_async_copy(cells_ref.at[part], held_ref.at[part, pl.ds(0, depth), :], sems.at[1 + p])
        copy.start()
        arrivals.append(copy)
    asked.wait()
    lower = lax.broadcasted_iota(jnp.int32, (ROWS, LANES), 0) < 4
    want = jnp.where(
        lower,
        jnp.broadcast_to(want_ref[0], (ROWS, LANES)),
        jnp.broadcast_to(want_ref[1], (ROWS, LANES)),
    ).astype(jnp.float32)
    for j in range(count):
        held_ref[j, depth : depth + ROWS, :] = want
    leaving = []
    for p in range(PIECES):
        part = pl.ds(p * group, group)
        arrivals[p].wait()
        copy = pltpu.make_async_copy(held_ref.at[part], out_ref.at[part], sems.at[1 + PIECES + p])
        copy.start()
        leaving.append(copy)
    for copy in leaving:
        copy.wait()


def source_kernel(gathered_ref, faces_ref, out_ref, held_ref, sems):
    depth = gathered_ref.shape[1] - ROWS
    slab = lax.axis_index("cell")
    slabs = faces_ref.shape[0] // ROWS
    span = depth // PIECES
    leaving = []

    def leave(k, first, size):
        part = pl.ds(first, size)
        copy = pltpu.make_async_copy(held_ref.at[:, part, :], out_ref.at[:, part, :], sems.at[k])
        copy.start()
        leaving.append(copy)

    def tile(ahead):
        place = (ahead & 3) * (slabs // 4) + (ahead >> 2)
        return faces_ref[pl.ds(pl.multiple_of(place * ROWS, ROWS), ROWS), :]

    wants = [gathered_ref[i, depth : depth + ROWS, :].astype(jnp.int32) for i in range(INST)]
    firsts = [want[0, 0] >> 7 for want in wants]

    for p in range(PIECES):
        for t in range(p * span, (p + 1) * span, ROWS):
            values = [gathered_ref[ORDER.index(i), t : t + ROWS, :] for i in range(INST)]
            outs = coupled(values[:ROTOR_INST], OMEGA_ROTOR) + coupled(values[ROTOR_INST:], OMEGA_STATOR)
            for i in range(INST):
                held_ref[ORDER.index(i), t : t + ROWS, :] = outs[i]
        if p < PIECES - 1:
            leave(p, p * span, span)
    for i, (want, first) in enumerate(zip(wants, firsts)):
        ahead = (first - slab) & (slabs - 1)
        place = want & (LANES - 1)
        here = jnp.take_along_axis(tile(ahead), place, axis=1, mode="promise_in_bounds")
        after = jnp.take_along_axis(tile((ahead + 1) & (slabs - 1)), place, axis=1, mode="promise_in_bounds")
        held_ref[i, depth : depth + ROWS, :] = jnp.where((want >> 7) == first, here, after)
    leave(PIECES - 1, depth - span, span + ROWS)
    for copy in leaving:
        copy.wait()


def fluxes(r, m, n, e):
    inv = 1.0 / r
    a = m * inv
    b = n * inv
    ma = m * a
    mb = m * b
    nb = n * b
    p = GAMMA_LESS * (e - 0.5 * (ma + nb))
    h = e + p
    return (m, ma + p, mb, h * a), (n, mb, nb + p, h * b)


def edge_kernel(cells_ref, export_ref, head_ref, tail_ref):
    axial = cells_ref.shape[1]
    rotor = lax.axis_index("inst") < ROTOR_INST
    for c in range(4):
        row = jnp.where(rotor, cells_ref[c, axial - 1 : axial, :], cells_ref[c, 0:1, :])
        export_ref[c : c + 1, :] = row
        export_ref[4 + c : 5 + c, :] = row
    lane = lax.broadcasted_iota(jnp.int32, (LANES, LANES), 1)
    for first in range(0, axial, LANES):
        span = pl.ds(first, LANES)
        sides = jnp.zeros((LANES, LANES), jnp.float32)
        for c in range(4):
            u = cells_ref[c, span, :]
            sides = jnp.where(lane == c, pltpu.roll(u, c, 1) if c else u, sides)
            sides = jnp.where(lane == 4 + c, pltpu.roll(u, 5 + c, 1), sides)
        sides = sides.T
        for ref, at, sign in ((head_ref, 0, -1.0), (tail_ref, 4, 1.0)):
            u = [sides[at + c : at + c + 1, :] for c in range(4)]
            _, flux_y = fluxes(*u)
            for c in range(4):
                ref[c : c + 1, span] = 0.5 * flux_y[c] + sign * DAMPING_COEF * u[c]


def partial_kernel(
    cur_ref, prev_ref, next_ref, right_ref, left_ref, out_ref, plus_ref, minus_ref, side_ref
):
    block = pl.program_id(0)
    last = pl.num_programs(0) - 1
    size = cur_ref.shape[1]
    rotor = lax.axis_index("inst") < ROTOR_INST

    def edge(outer, own, at_end):
        return [jnp.where(at_end, jnp.broadcast_to(own[c], (ROWS, LANES)), outer[c]) for c in range(4)]

    before = edge([prev_ref[c] for c in range(4)], [cur_ref[c, 0:1, :] for c in range(4)], block == 0)
    after = edge(
        [next_ref[c] for c in range(4)], [cur_ref[c, size - 1 : size, :] for c in range(4)], block == last
    )
    keep_before = jnp.where(jnp.logical_or(block > 0, rotor), 1.0, 0.0)
    keep_after = jnp.where(jnp.logical_and(block == last, rotor), 0.0, 1.0)
    flux_before, _ = fluxes(*before)
    flux_after, _ = fluxes(*after)
    for c in range(4):
        minus_ref[c, 0:ROWS, :] = keep_before * (0.5 * flux_before[c] + DAMPING_COEF * before[c])
        plus_ref[c, size + ROWS : size + 2 * ROWS, :] = keep_after * (
            0.5 * flux_after[c] - DAMPING_COEF * after[c]
        )

    lane = lax.broadcasted_iota(jnp.int32, (ROWS, LANES), 1)
    sides = jnp.concatenate([right_ref[...], left_ref[...], jnp.zeros((LANES - 8, LANES), jnp.float32)], 0)
    side_ref[...] = sides.T

    def first(t, carry):
        rows = pl.ds(pl.multiple_of(t * ROWS, ROWS), ROWS)
        shifted = pl.ds(pl.multiple_of(t * ROWS + ROWS, ROWS), ROWS)
        u = [cur_ref[c, rows, :] for c in range(4)]
        flux_x, flux_y = fluxes(*u)
        side = side_ref[rows, :]
        for c in range(4):
            half_x = 0.5 * flux_x[c]
            half_y = 0.5 * flux_y[c]
            damped = DAMPING_COEF * u[c]
            plus_ref[c, shifted, :] = half_x - damped
            minus_ref[c, shifted, :] = half_x + damped
            up = jnp.where(lane == 0, jnp.broadcast_to(side[:, c : c + 1], (ROWS, LANES)), half_y - damped)
            down = jnp.where(lane == LANES - 1, jnp.broadcast_to(side[:, 4 + c : 5 + c], (ROWS, LANES)), half_y + damped)
            out_ref[c, rows, :] = (
                pltpu.roll(up, LANES - 1, 1) - pltpu.roll(down, 1, 1) + (4.0 * DAMPING_COEF) * u[c]
            )
        return carry

    lax.fori_loop(0, size // ROWS, first, 0, unroll=4)

    for t in range(size // ROWS):
        lo = t * ROWS
        for c in range(4):
            out_ref[c, lo : lo + ROWS, :] = (
                out_ref[c, lo : lo + ROWS, :]
                + plus_ref[c, lo + ROWS + 1 : lo + 2 * ROWS + 1, :]
                - minus_ref[c, lo + ROWS - 1 : lo + 2 * ROWS - 1, :]
            )


def finish_kernel(
    packed_ref, partial_ref, cells_ref, inst_ref, weight_ref, residual_ref, new_ref, res_ref, next_ref, sems
):
    rotor = lax.axis_index("inst") < ROTOR_INST
    axial = cells_ref.shape[1]
    depth = packed_ref.shape[1] - ROWS
    per = axial // depth
    row = lax.broadcasted_iota(jnp.int32, (ROWS, LANES), 0)
    lower = row < 4

    def spread(ref, first, second):
        return jnp.where(
            lower,
            jnp.broadcast_to(ref[first : first + 1, :], (ROWS, LANES)),
            jnp.broadcast_to(ref[second : second + 1, :], (ROWS, LANES)),
        )

    inst0, inst2 = spread(inst_ref, 0, 1), spread(inst_ref, 2, 3)
    weight0, weight2 = spread(weight_ref, 0, 1), spread(weight_ref, 2, 3)
    total = jnp.zeros((ROWS, LANES), jnp.float32)
    for i in range(INST):
        coef = jnp.where(inst0 == i, weight0, 0.0) + jnp.where(inst2 == i, weight2, 0.0)
        total = total + coef * packed_ref[ORDER.index(i), depth : depth + ROWS, :]
    ghost = total + pltpu.roll(total, 4, 0)
    ghost = [jnp.broadcast_to(ghost[c : c + 1, :], (ROWS, LANES)) for c in range(4)]
    flux_x, _ = fluxes(*ghost)
    head = jnp.logical_and(row == 0, jnp.logical_not(rotor))
    tail = jnp.logical_and(row == ROWS - 1, rotor)
    copies = []
    for c in range(4):
        half, damped = 0.5 * flux_x[c], DAMPING_COEF * ghost[c]
        at_head = jnp.where(head, -half - damped, 0.0)
        at_tail = jnp.where(tail, half - damped, 0.0)
        for j in range(per):

            def strip(t, carry, c=c, j=j):
                rows = pl.ds(pl.multiple_of(j * depth + t * ROWS, ROWS), ROWS)
                mine = pl.ds(pl.multiple_of(t * ROWS, ROWS), ROWS)
                out = partial_ref[c, rows, :] + packed_ref[c * per + j, mine, :]
                res_ref[c, rows, :] = out
                next_ref[c, rows, :] = cells_ref[c, rows, :] - PSEUDO_STEP * out
                return carry

            lax.fori_loop(0, depth // ROWS, strip, 0, unroll=True)
        for first, extra in ((0, at_head), (axial - ROWS, at_tail)):
            out = res_ref[c, first : first + ROWS, :] + extra
            res_ref[c, first : first + ROWS, :] = out
            next_ref[c, first : first + ROWS, :] = cells_ref[c, first : first + ROWS, :] - PSEUDO_STEP * out
        for k, (src, dst) in enumerate(((res_ref, residual_ref), (next_ref, new_ref))):
            copy = pltpu.make_async_copy(src.at[c], dst.at[c], sems.at[2 * c + k])
            copy.start()
            copies.append(copy)
    for copy in copies:
        copy.wait()


def collected(block, axis):
    count = lax.axis_size(axis)
    for step in (count // 4, 1):
        blocks = [block]
        for k in range(1, 4):
            pairs = [((i + k * step) % count, i) for i in range(count)]
            blocks.append(lax.ppermute(block, axis, pairs))
        block = jnp.concatenate(blocks, 0)
    return block


def on_device(state, src_inst, src_face, weights):
    cells = state[0]
    axial, width = cells.shape[1], cells.shape[2]
    inst_count = lax.axis_size("inst")
    cell_count = lax.axis_size("cell")
    depth = 4 * axial // inst_count

    vmem = pl.BlockSpec(memory_space=pltpu.VMEM)
    anywhere = pl.BlockSpec(memory_space=pl.ANY)
    sent = pl.pallas_call(
        send_kernel,
        out_shape=jax.ShapeDtypeStruct((inst_count, depth + ROWS, width), jnp.float32),
        in_specs=[anywhere, anywhere],
        out_specs=anywhere,
        scratch_shapes=[
            pltpu.VMEM((inst_count, depth + ROWS, width), jnp.float32),
            pltpu.VMEM(src_face.shape, jnp.int32),
            pltpu.SemaphoreType.DMA((1 + 2 * PIECES,)),
        ],
        compiler_params=pltpu.CompilerParams(vmem_limit_bytes=60 << 20),
        name="send",
    )(cells.reshape(inst_count, depth, width), src_face)
    sent, cells = lax.optimization_barrier((sent, cells))
    export, head, tail = pl.pallas_call(
        edge_kernel,
        out_shape=[
            jax.ShapeDtypeStruct((ROWS, width), jnp.float32),
            jax.ShapeDtypeStruct((4, axial), jnp.float32),
            jax.ShapeDtypeStruct((4, axial), jnp.float32),
        ],
        in_specs=[vmem],
        out_specs=[vmem] * 3,
        compiler_params=pltpu.CompilerParams(vmem_limit_bytes=16 << 20),
        cost_estimate=pl.CostEstimate(flops=0, bytes_accessed=32 << 20, transcendentals=0),
        name="edges",
    )(cells)
    gathered = lax.all_to_all(sent, "inst", 0, 0, axis_index_groups=[ORDER])
    faces = collected(export, "cell")
    packed = pl.pallas_call(
        source_kernel,
        out_shape=jax.ShapeDtypeStruct((inst_count, depth + ROWS, width), jnp.float32),
        in_specs=[vmem, vmem],
        out_specs=anywhere,
        scratch_shapes=[
            pltpu.VMEM((inst_count, depth + ROWS, width), jnp.float32),
            pltpu.SemaphoreType.DMA((PIECES,)),
        ],
        compiler_params=pltpu.CompilerParams(vmem_limit_bytes=16 << 20),
        name="source",
    )(gathered, faces)
    head, tail, packed = lax.optimization_barrier((head, tail, packed))
    packed = lax.all_to_all(packed, "inst", 0, 0, axis_index_groups=[ORDER])

    right = lax.ppermute(head, "cell", [((i + 1) % cell_count, i) for i in range(cell_count)])
    left = lax.ppermute(tail, "cell", [(i, (i + 1) % cell_count) for i in range(cell_count)])

    blocks = axial // depth
    per = depth // ROWS
    strips = axial // ROWS
    block_spec = pl.BlockSpec((4, depth, width), lambda g: (0, g, 0))
    halo_spec = pl.BlockSpec((4, depth), lambda g: (0, g))
    partial = pl.pallas_call(
        partial_kernel,
        grid=(blocks,),
        out_shape=pltpu.VMEM(cells.shape, jnp.float32),
        in_specs=[
            block_spec,
            pl.BlockSpec((4, ROWS, width), lambda g: (0, jnp.maximum(g * per - 1, 0), 0)),
            pl.BlockSpec((4, ROWS, width), lambda g: (0, jnp.minimum(g * per + per, strips - 1), 0)),
            halo_spec,
            halo_spec,
        ],
        out_specs=block_spec,
        scratch_shapes=[
            pltpu.VMEM((4, depth + 2 * ROWS, width), jnp.float32),
            pltpu.VMEM((4, depth + 2 * ROWS, width), jnp.float32),
            pltpu.VMEM((depth, width), jnp.float32),
        ],
        compiler_params=pltpu.CompilerParams(vmem_limit_bytes=16 << 20),
        cost_estimate=pl.CostEstimate(flops=100 * cells.size, bytes_accessed=16 * cells.size, transcendentals=0),
        name="partial",
    )(cells, cells, cells, right, left)
    residual, new_state = pl.pallas_call(
        finish_kernel,
        out_shape=[jax.ShapeDtypeStruct(cells.shape, jnp.float32)] * 2,
        in_specs=[vmem] * 5,
        out_specs=[anywhere, anywhere],
        scratch_shapes=[
            pltpu.VMEM(cells.shape, jnp.float32),
            pltpu.VMEM(cells.shape, jnp.float32),
            pltpu.SemaphoreType.DMA((8,)),
        ],
        compiler_params=pltpu.CompilerParams(vmem_limit_bytes=16 << 20),
        name="finish",
    )(packed, partial, cells, src_inst[:, 0, :], weights[:, 0, :])
    return residual[None], new_state[None]


def solution(mesh):
    return jax.shard_map(
        on_device,
        mesh=mesh,
        in_specs=(
            P("inst", None, None, "cell"),
            P(None, "inst", "cell"),
            P(None, "inst", "cell"),
            P(None, "inst", "cell"),
        ),
        out_specs=(P("inst", None, None, "cell"), P("inst", None, None, "cell")),
        check_vma=False,
    )
```

```python
import jax
import jax.numpy as jnp
import numpy as np
from jax import lax
from jax.experimental import pallas as pl
from jax.experimental.pallas import tpu as pltpu
from jax.sharding import PartitionSpec as P

ROTOR_INST = 9
STATOR_INST = 7
INST = ROTOR_INST + STATOR_INST
OMEGA_ROTOR = 0.8
OMEGA_STATOR = 0.6
GAMMA_LESS = 0.4
DAMPING_COEF = 0.05
PSEUDO_STEP = 0.2
LANES = 128
ROWS = 8
PIECES = 4
ORDER = (8, 12, 3, 4, 6, 15, 10, 14, 13, 1, 9, 2, 5, 7, 0, 11)


def pitch_coefficients(count, omega):
    steps = np.arange(1, (count - 1) // 2 + 1)
    return omega * 0.5 * np.power(-1.0, steps) / np.sin(np.pi * steps / count)


def coupled(values, omega):
    count = len(values)
    coefs = pitch_coefficients(count, omega)
    outs = []
    for i in range(count):
        total = None
        for d, coef in enumerate(coefs, 1):
            term = float(coef) * (values[(i - d) % count] - values[(i + d) % count])
            total = term if total is None else total + term
        outs.append(total)
    return outs


def send_kernel(cells_ref, face_ref, out_ref, held_ref, want_ref, sems):
    count, depth = out_ref.shape[0], out_ref.shape[1] - ROWS
    group = count // PIECES
    asked = pltpu.make_async_copy(face_ref, want_ref, sems.at[0])
    asked.start()
    arrivals = []
    for p in range(PIECES):
        part = pl.ds(p * group, group)
        copy = pltpu.make_async_copy(cells_ref.at[part], held_ref.at[part, pl.ds(0, depth), :], sems.at[1 + p])
        copy.start()
        arrivals.append(copy)
    asked.wait()
    lower = lax.broadcasted_iota(jnp.int32, (ROWS, LANES), 0) < 4
    want = jnp.where(
        lower,
        jnp.broadcast_to(want_ref[0], (ROWS, LANES)),
        jnp.broadcast_to(want_ref[1], (ROWS, LANES)),
    ).astype(jnp.float32)
    for j in range(count):
        held_ref[j, depth : depth + ROWS, :] = want
    leaving = []
    for p in range(PIECES):
        part = pl.ds(p * group, group)
        arrivals[p].wait()
        copy = pltpu.make_async_copy(held_ref.at[part], out_ref.at[part], sems.at[1 + PIECES + p])
        copy.start()
        leaving.append(copy)
    for copy in leaving:
        copy.wait()


def source_kernel(gathered_ref, faces_ref, out_ref, held_ref, sems):
    depth = gathered_ref.shape[1] - ROWS
    slab = lax.axis_index("cell")
    slabs = faces_ref.shape[0] // ROWS
    span = depth // PIECES
    leaving = []

    def leave(k, first, size):
        part = pl.ds(first, size)
        copy = pltpu.make_async_copy(held_ref.at[:, part, :], out_ref.at[:, part, :], sems.at[k])
        copy.start()
        leaving.append(copy)

    def tile(ahead):
        place = ahead
        return faces_ref[pl.ds(pl.multiple_of(place * ROWS, ROWS), ROWS), :]

    wants = [gathered_ref[i, depth : depth + ROWS, :].astype(jnp.int32) for i in range(INST)]
    firsts = [want[0, 0] >> 7 for want in wants]

    for p in range(PIECES):
        for t in range(p * span, (p + 1) * span, ROWS):
            values = [gathered_ref[ORDER.index(i), t : t + ROWS, :] for i in range(INST)]
            outs = coupled(values[:ROTOR_INST], OMEGA_ROTOR) + coupled(values[ROTOR_INST:], OMEGA_STATOR)
            for i in range(INST):
                held_ref[ORDER.index(i), t : t + ROWS, :] = outs[i]
        if p < PIECES - 1:
            leave(p, p * span, span)
    for i, (want, first) in enumerate(zip(wants, firsts)):
        ahead = (first - slab) & (slabs - 1)
        place = want & (LANES - 1)
        here = jnp.take_along_axis(tile(ahead), place, axis=1, mode="promise_in_bounds")
        after = jnp.take_along_axis(tile((ahead + 1) & (slabs - 1)), place, axis=1, mode="promise_in_bounds")
        held_ref[i, depth : depth + ROWS, :] = jnp.where((want >> 7) == first, here, after)
    leave(PIECES - 1, depth - span, span + ROWS)
    for copy in leaving:
        copy.wait()


def fluxes(r, m, n, e):
    inv = 1.0 / r
    a = m * inv
    b = n * inv
    ma = m * a
    mb = m * b
    nb = n * b
    p = GAMMA_LESS * (e - 0.5 * (ma + nb))
    h = e + p
    return (m, ma + p, mb, h * a), (n, mb, nb + p, h * b)


def edge_kernel(cells_ref, export_ref, head_ref, tail_ref):
    axial = cells_ref.shape[1]
    rotor = lax.axis_index("inst") < ROTOR_INST
    for c in range(4):
        row = jnp.where(rotor, cells_ref[c, axial - 1 : axial, :], cells_ref[c, 0:1, :])
        export_ref[c : c + 1, :] = row
        export_ref[4 + c : 5 + c, :] = row
    lane = lax.broadcasted_iota(jnp.int32, (LANES, LANES), 1)
    for first in range(0, axial, LANES):
        span = pl.ds(first, LANES)
        sides = jnp.zeros((LANES, LANES), jnp.float32)
        for c in range(4):
            u = cells_ref[c, span, :]
            sides = jnp.where(lane == c, pltpu.roll(u, c, 1) if c else u, sides)
            sides = jnp.where(lane == 4 + c, pltpu.roll(u, 5 + c, 1), sides)
        sides = sides.T
        for ref, at, sign in ((head_ref, 0, -1.0), (tail_ref, 4, 1.0)):
            u = [sides[at + c : at + c + 1, :] for c in range(4)]
            _, flux_y = fluxes(*u)
            for c in range(4):
                ref[c : c + 1, span] = 0.5 * flux_y[c] + sign * DAMPING_COEF * u[c]


def partial_kernel(
    cur_ref, prev_ref, next_ref, right_ref, left_ref, out_ref, plus_ref, minus_ref, side_ref
):
    block = pl.program_id(0)
    last = pl.num_programs(0) - 1
    size = cur_ref.shape[1]
    rotor = lax.axis_index("inst") < ROTOR_INST

    def edge(outer, own, at_end):
        return [jnp.where(at_end, jnp.broadcast_to(own[c], (ROWS, LANES)), outer[c]) for c in range(4)]

    before = edge([prev_ref[c] for c in range(4)], [cur_ref[c, 0:1, :] for c in range(4)], block == 0)
    after = edge(
        [next_ref[c] for c in range(4)], [cur_ref[c, size - 1 : size, :] for c in range(4)], block == last
    )
    keep_before = jnp.where(jnp.logical_or(block > 0, rotor), 1.0, 0.0)
    keep_after = jnp.where(jnp.logical_and(block == last, rotor), 0.0, 1.0)
    flux_before, _ = fluxes(*before)
    flux_after, _ = fluxes(*after)
    for c in range(4):
        minus_ref[c, 0:ROWS, :] = keep_before * (0.5 * flux_before[c] + DAMPING_COEF * before[c])
        plus_ref[c, size + ROWS : size + 2 * ROWS, :] = keep_after * (
            0.5 * flux_after[c] - DAMPING_COEF * after[c]
        )

    lane = lax.broadcasted_iota(jnp.int32, (ROWS, LANES), 1)
    sides = jnp.concatenate([right_ref[...], left_ref[...], jnp.zeros((LANES - 8, LANES), jnp.float32)], 0)
    side_ref[...] = sides.T

    def first(t, carry):
        rows = pl.ds(pl.multiple_of(t * ROWS, ROWS), ROWS)
        shifted = pl.ds(pl.multiple_of(t * ROWS + ROWS, ROWS), ROWS)
        u = [cur_ref[c, rows, :] for c in range(4)]
        flux_x, flux_y = fluxes(*u)
        side = side_ref[rows, :]
        for c in range(4):
            half_x = 0.5 * flux_x[c]
            half_y = 0.5 * flux_y[c]
            damped = DAMPING_COEF * u[c]
            plus_ref[c, shifted, :] = half_x - damped
            minus_ref[c, shifted, :] = half_x + damped
            up = jnp.where(lane == 0, jnp.broadcast_to(side[:, c : c + 1], (ROWS, LANES)), half_y - damped)
            down = jnp.where(lane == LANES - 1, jnp.broadcast_to(side[:, 4 + c : 5 + c], (ROWS, LANES)), half_y + damped)
            out_ref[c, rows, :] = (
                pltpu.roll(up, LANES - 1, 1) - pltpu.roll(down, 1, 1) + (4.0 * DAMPING_COEF) * u[c]
            )
        return carry

    lax.fori_loop(0, size // ROWS, first, 0, unroll=4)

    for t in range(size // ROWS):
        lo = t * ROWS
        for c in range(4):
            out_ref[c, lo : lo + ROWS, :] = (
                out_ref[c, lo : lo + ROWS, :]
                + plus_ref[c, lo + ROWS + 1 : lo + 2 * ROWS + 1, :]
                - minus_ref[c, lo + ROWS - 1 : lo + 2 * ROWS - 1, :]
            )


def finish_kernel(
    packed_ref, partial_ref, cells_ref, inst_ref, weight_ref, residual_ref, new_ref, res_ref, next_ref, sems
):
    rotor = lax.axis_index("inst") < ROTOR_INST
    axial = cells_ref.shape[1]
    depth = packed_ref.shape[1] - ROWS
    per = axial // depth
    row = lax.broadcasted_iota(jnp.int32, (ROWS, LANES), 0)
    lower = row < 4

    def spread(ref, first, second):
        return jnp.where(
            lower,
            jnp.broadcast_to(ref[first : first + 1, :], (ROWS, LANES)),
            jnp.broadcast_to(ref[second : second + 1, :], (ROWS, LANES)),
        )

    inst0, inst2 = spread(inst_ref, 0, 1), spread(inst_ref, 2, 3)
    weight0, weight2 = spread(weight_ref, 0, 1), spread(weight_ref, 2, 3)
    total = jnp.zeros((ROWS, LANES), jnp.float32)
    for i in range(INST):
        coef = jnp.where(inst0 == i, weight0, 0.0) + jnp.where(inst2 == i, weight2, 0.0)
        total = total + coef * packed_ref[ORDER.index(i), depth : depth + ROWS, :]
    ghost = total + pltpu.roll(total, 4, 0)
    ghost = [jnp.broadcast_to(ghost[c : c + 1, :], (ROWS, LANES)) for c in range(4)]
    flux_x, _ = fluxes(*ghost)
    head = jnp.logical_and(row == 0, jnp.logical_not(rotor))
    tail = jnp.logical_and(row == ROWS - 1, rotor)
    copies = []
    for c in range(4):
        half, damped = 0.5 * flux_x[c], DAMPING_COEF * ghost[c]
        at_head = jnp.where(head, -half - damped, 0.0)
        at_tail = jnp.where(tail, half - damped, 0.0)
        for j in range(per):

            def strip(t, carry, c=c, j=j):
                rows = pl.ds(pl.multiple_of(j * depth + t * ROWS, ROWS), ROWS)
                mine = pl.ds(pl.multiple_of(t * ROWS, ROWS), ROWS)
                out = partial_ref[c, rows, :] + packed_ref[c * per + j, mine, :]
                res_ref[c, rows, :] = out
                next_ref[c, rows, :] = cells_ref[c, rows, :] - PSEUDO_STEP * out
                return carry

            lax.fori_loop(0, depth // ROWS, strip, 0, unroll=True)
        for first, extra in ((0, at_head), (axial - ROWS, at_tail)):
            out = res_ref[c, first : first + ROWS, :] + extra
            res_ref[c, first : first + ROWS, :] = out
            next_ref[c, first : first + ROWS, :] = cells_ref[c, first : first + ROWS, :] - PSEUDO_STEP * out
        for k, (src, dst) in enumerate(((res_ref, residual_ref), (next_ref, new_ref))):
            copy = pltpu.make_async_copy(src.at[c], dst.at[c], sems.at[2 * c + k])
            copy.start()
            copies.append(copy)
    for copy in copies:
        copy.wait()


def collected(block, axis):
    count = lax.axis_size(axis)
    for step in (1, count // 4):
        blocks = [block]
        for k in range(1, 4):
            pairs = [((i + k * step) % count, i) for i in range(count)]
            blocks.append(lax.ppermute(block, axis, pairs))
        block = jnp.concatenate(blocks, 0)
    return block


def on_device(state, src_inst, src_face, weights):
    cells = state[0]
    axial, width = cells.shape[1], cells.shape[2]
    inst_count = lax.axis_size("inst")
    cell_count = lax.axis_size("cell")
    depth = 4 * axial // inst_count

    vmem = pl.BlockSpec(memory_space=pltpu.VMEM)
    anywhere = pl.BlockSpec(memory_space=pl.ANY)
    sent = pl.pallas_call(
        send_kernel,
        out_shape=jax.ShapeDtypeStruct((inst_count, depth + ROWS, width), jnp.float32),
        in_specs=[anywhere, anywhere],
        out_specs=anywhere,
        scratch_shapes=[
            pltpu.VMEM((inst_count, depth + ROWS, width), jnp.float32),
            pltpu.VMEM(src_face.shape, jnp.int32),
            pltpu.SemaphoreType.DMA((1 + 2 * PIECES,)),
        ],
        compiler_params=pltpu.CompilerParams(vmem_limit_bytes=60 << 20),
        name="send",
    )(cells.reshape(inst_count, depth, width), src_face)
    sent, cells = lax.optimization_barrier((sent, cells))
    export, head, tail = pl.pallas_call(
        edge_kernel,
        out_shape=[
            jax.ShapeDtypeStruct((ROWS, width), jnp.float32),
            jax.ShapeDtypeStruct((4, axial), jnp.float32),
            jax.ShapeDtypeStruct((4, axial), jnp.float32),
        ],
        in_specs=[vmem],
        out_specs=[vmem] * 3,
        compiler_params=pltpu.CompilerParams(vmem_limit_bytes=16 << 20),
        cost_estimate=pl.CostEstimate(flops=0, bytes_accessed=32 << 20, transcendentals=0),
        name="edges",
    )(cells)
    gathered = lax.all_to_all(sent, "inst", 0, 0, axis_index_groups=[ORDER])
    faces = collected(export[:4], "cell").reshape(cell_count, 4, width)
    faces = jnp.concatenate([faces, faces], 1).reshape(cell_count * ROWS, width)
    packed = pl.pallas_call(
        source_kernel,
        out_shape=jax.ShapeDtypeStruct((inst_count, depth + ROWS, width), jnp.float32),
        in_specs=[vmem, vmem],
        out_specs=anywhere,
        scratch_shapes=[
            pltpu.VMEM((inst_count, depth + ROWS, width), jnp.float32),
            pltpu.SemaphoreType.DMA((PIECES,)),
        ],
        compiler_params=pltpu.CompilerParams(vmem_limit_bytes=16 << 20),
        name="source",
    )(gathered, faces)
    head, tail, packed = lax.optimization_barrier((head, tail, packed))
    packed = lax.all_to_all(packed, "inst", 0, 0, axis_index_groups=[ORDER])

    right = lax.ppermute(head, "cell", [((i + 1) % cell_count, i) for i in range(cell_count)])
    left = lax.ppermute(tail, "cell", [(i, (i + 1) % cell_count) for i in range(cell_count)])

    blocks = axial // depth
    per = depth // ROWS
    strips = axial // ROWS
    block_spec = pl.BlockSpec((4, depth, width), lambda g: (0, g, 0))
    halo_spec = pl.BlockSpec((4, depth), lambda g: (0, g))
    partial = pl.pallas_call(
        partial_kernel,
        grid=(blocks,),
        out_shape=pltpu.VMEM(cells.shape, jnp.float32),
        in_specs=[
            block_spec,
            pl.BlockSpec((4, ROWS, width), lambda g: (0, jnp.maximum(g * per - 1, 0), 0)),
            pl.BlockSpec((4, ROWS, width), lambda g: (0, jnp.minimum(g * per + per, strips - 1), 0)),
            halo_spec,
            halo_spec,
        ],
        out_specs=block_spec,
        scratch_shapes=[
            pltpu.VMEM((4, depth + 2 * ROWS, width), jnp.float32),
            pltpu.VMEM((4, depth + 2 * ROWS, width), jnp.float32),
            pltpu.VMEM((depth, width), jnp.float32),
        ],
        compiler_params=pltpu.CompilerParams(vmem_limit_bytes=16 << 20),
        cost_estimate=pl.CostEstimate(flops=100 * cells.size, bytes_accessed=16 * cells.size, transcendentals=0),
        name="partial",
    )(cells, cells, cells, right, left)
    residual, new_state = pl.pallas_call(
        finish_kernel,
        out_shape=[jax.ShapeDtypeStruct(cells.shape, jnp.float32)] * 2,
        in_specs=[vmem] * 5,
        out_specs=[anywhere, anywhere],
        scratch_shapes=[
            pltpu.VMEM(cells.shape, jnp.float32),
            pltpu.VMEM(cells.shape, jnp.float32),
            pltpu.SemaphoreType.DMA((8,)),
        ],
        compiler_params=pltpu.CompilerParams(vmem_limit_bytes=16 << 20),
        name="finish",
    )(packed, partial, cells, src_inst[:, 0, :], weights[:, 0, :])
    return residual[None], new_state[None]


def solution(mesh):
    return jax.shard_map(
        on_device,
        mesh=mesh,
        in_specs=(
            P("inst", None, None, "cell"),
            P(None, "inst", "cell"),
            P(None, "inst", "cell"),
            P(None, "inst", "cell"),
        ),
        out_specs=(P("inst", None, None, "cell"), P("inst", None, None, "cell")),
        check_vma=False,
    )
```

```python
import jax
import jax.numpy as jnp
import numpy as np
from jax import lax
from jax.experimental import pallas as pl
from jax.experimental.pallas import tpu as pltpu
from jax.sharding import PartitionSpec as P

ROTOR_INST = 9
STATOR_INST = 7
INST = ROTOR_INST + STATOR_INST
OMEGA_ROTOR = 0.8
OMEGA_STATOR = 0.6
GAMMA_LESS = 0.4
DAMPING_COEF = 0.05
PSEUDO_STEP = 0.2
LANES = 128
ROWS = 8
PIECES = 4
SPREAD = (8, 12, 3, 4, 6, 15, 10, 14, 13, 1, 9, 2, 5, 7, 0, 11)
COLLECT = (0, 4, 8, 12, 2, 6, 10, 14, 1, 5, 9, 13, 3, 7, 11, 15)


def pitch_coefficients(count, omega):
    steps = np.arange(1, (count - 1) // 2 + 1)
    return omega * 0.5 * np.power(-1.0, steps) / np.sin(np.pi * steps / count)


def coupled(values, omega):
    count = len(values)
    coefs = pitch_coefficients(count, omega)
    outs = []
    for i in range(count):
        total = None
        for d, coef in enumerate(coefs, 1):
            term = float(coef) * (values[(i - d) % count] - values[(i + d) % count])
            total = term if total is None else total + term
        outs.append(total)
    return outs


def send_kernel(cells_ref, face_ref, out_ref, held_ref, want_ref, sems):
    count, depth = out_ref.shape[0], out_ref.shape[1] - ROWS
    group = count // PIECES
    asked = pltpu.make_async_copy(face_ref, want_ref, sems.at[0])
    asked.start()
    arrivals = []
    for p in range(PIECES):
        part = pl.ds(p * group, group)
        copy = pltpu.make_async_copy(cells_ref.at[part], held_ref.at[part, pl.ds(0, depth), :], sems.at[1 + p])
        copy.start()
        arrivals.append(copy)
    asked.wait()
    lower = lax.broadcasted_iota(jnp.int32, (ROWS, LANES), 0) < 4
    want = jnp.where(
        lower,
        jnp.broadcast_to(want_ref[0], (ROWS, LANES)),
        jnp.broadcast_to(want_ref[1], (ROWS, LANES)),
    ).astype(jnp.float32)
    for j in range(count):
        held_ref[j, depth : depth + ROWS, :] = want
    leaving = []
    for p in range(PIECES):
        part = pl.ds(p * group, group)
        arrivals[p].wait()
        copy = pltpu.make_async_copy(held_ref.at[part], out_ref.at[part], sems.at[1 + PIECES + p])
        copy.start()
        leaving.append(copy)
    for copy in leaving:
        copy.wait()


def source_kernel(gathered_ref, faces_ref, out_ref, held_ref, sems):
    depth = gathered_ref.shape[1] - ROWS
    slab = lax.axis_index("cell")
    slabs = faces_ref.shape[0] // ROWS
    span = depth // PIECES
    leaving = []

    def leave(k, first, size):
        part = pl.ds(first, size)
        copy = pltpu.make_async_copy(held_ref.at[:, part, :], out_ref.at[:, part, :], sems.at[k])
        copy.start()
        leaving.append(copy)

    def tile(ahead):
        place = ahead
        return faces_ref[pl.ds(pl.multiple_of(place * ROWS, ROWS), ROWS), :]

    wants = [gathered_ref[i, depth : depth + ROWS, :].astype(jnp.int32) for i in range(INST)]
    firsts = [want[0, 0] >> 7 for want in wants]

    for p in range(PIECES):
        for t in range(p * span, (p + 1) * span, ROWS):
            values = [gathered_ref[SPREAD.index(i), t : t + ROWS, :] for i in range(INST)]
            outs = coupled(values[:ROTOR_INST], OMEGA_ROTOR) + coupled(values[ROTOR_INST:], OMEGA_STATOR)
            for i in range(INST):
                held_ref[COLLECT.index(i), t : t + ROWS, :] = outs[i]
        if p < PIECES - 1:
            leave(p, p * span, span)
    for i, (want, first) in enumerate(zip(wants, firsts)):
        ahead = (first - slab) & (slabs - 1)
        place = want & (LANES - 1)
        here = jnp.take_along_axis(tile(ahead), place, axis=1, mode="promise_in_bounds")
        after = jnp.take_along_axis(tile((ahead + 1) & (slabs - 1)), place, axis=1, mode="promise_in_bounds")
        held_ref[COLLECT.index(SPREAD[i]), depth : depth + ROWS, :] = jnp.where((want >> 7) == first, here, after)
    leave(PIECES - 1, depth - span, span + ROWS)
    for copy in leaving:
        copy.wait()


def fluxes(r, m, n, e):
    inv = 1.0 / r
    a = m * inv
    b = n * inv
    ma = m * a
    mb = m * b
    nb = n * b
    p = GAMMA_LESS * (e - 0.5 * (ma + nb))
    h = e + p
    return (m, ma + p, mb, h * a), (n, mb, nb + p, h * b)


def edge_kernel(cells_ref, head_ref, tail_ref):
    axial = cells_ref.shape[1]
    lane = lax.broadcasted_iota(jnp.int32, (LANES, LANES), 1)
    for first in range(0, axial, LANES):
        span = pl.ds(first, LANES)
        sides = jnp.zeros((LANES, LANES), jnp.float32)
        for c in range(4):
            u = cells_ref[c, span, :]
            sides = jnp.where(lane == c, pltpu.roll(u, c, 1) if c else u, sides)
            sides = jnp.where(lane == 4 + c, pltpu.roll(u, 5 + c, 1), sides)
        sides = sides.T
        for ref, at, sign in ((head_ref, 0, -1.0), (tail_ref, 4, 1.0)):
            u = [sides[at + c : at + c + 1, :] for c in range(4)]
            _, flux_y = fluxes(*u)
            for c in range(4):
                ref[c : c + 1, span] = 0.5 * flux_y[c] + sign * DAMPING_COEF * u[c]


def partial_kernel(
    cur_ref, prev_ref, next_ref, right_ref, left_ref, out_ref, plus_ref, minus_ref, side_ref
):
    block = pl.program_id(0)
    last = pl.num_programs(0) - 1
    size = cur_ref.shape[1]
    rotor = lax.axis_index("inst") < ROTOR_INST

    def edge(outer, own, at_end):
        return [jnp.where(at_end, jnp.broadcast_to(own[c], (ROWS, LANES)), outer[c]) for c in range(4)]

    before = edge([prev_ref[c] for c in range(4)], [cur_ref[c, 0:1, :] for c in range(4)], block == 0)
    after = edge(
        [next_ref[c] for c in range(4)], [cur_ref[c, size - 1 : size, :] for c in range(4)], block == last
    )
    keep_before = jnp.where(jnp.logical_or(block > 0, rotor), 1.0, 0.0)
    keep_after = jnp.where(jnp.logical_and(block == last, rotor), 0.0, 1.0)
    flux_before, _ = fluxes(*before)
    flux_after, _ = fluxes(*after)
    for c in range(4):
        minus_ref[c, 0:ROWS, :] = keep_before * (0.5 * flux_before[c] + DAMPING_COEF * before[c])
        plus_ref[c, size + ROWS : size + 2 * ROWS, :] = keep_after * (
            0.5 * flux_after[c] - DAMPING_COEF * after[c]
        )

    lane = lax.broadcasted_iota(jnp.int32, (ROWS, LANES), 1)
    sides = jnp.concatenate([right_ref[...], left_ref[...], jnp.zeros((LANES - 8, LANES), jnp.float32)], 0)
    side_ref[...] = sides.T

    def first(t, carry):
        rows = pl.ds(pl.multiple_of(t * ROWS, ROWS), ROWS)
        shifted = pl.ds(pl.multiple_of(t * ROWS + ROWS, ROWS), ROWS)
        u = [cur_ref[c, rows, :] for c in range(4)]
        flux_x, flux_y = fluxes(*u)
        side = side_ref[rows, :]
        for c in range(4):
            half_x = 0.5 * flux_x[c]
            half_y = 0.5 * flux_y[c]
            damped = DAMPING_COEF * u[c]
            plus_ref[c, shifted, :] = half_x - damped
            minus_ref[c, shifted, :] = half_x + damped
            up = jnp.where(lane == 0, jnp.broadcast_to(side[:, c : c + 1], (ROWS, LANES)), half_y - damped)
            down = jnp.where(lane == LANES - 1, jnp.broadcast_to(side[:, 4 + c : 5 + c], (ROWS, LANES)), half_y + damped)
            out_ref[c, rows, :] = (
                pltpu.roll(up, LANES - 1, 1) - pltpu.roll(down, 1, 1) + (4.0 * DAMPING_COEF) * u[c]
            )
        return carry

    lax.fori_loop(0, size // ROWS, first, 0, unroll=4)

    for t in range(size // ROWS):
        lo = t * ROWS
        for c in range(4):
            out_ref[c, lo : lo + ROWS, :] = (
                out_ref[c, lo : lo + ROWS, :]
                + plus_ref[c, lo + ROWS + 1 : lo + 2 * ROWS + 1, :]
                - minus_ref[c, lo + ROWS - 1 : lo + 2 * ROWS - 1, :]
            )


def finish_kernel(
    packed_ref, partial_ref, cells_ref, inst_ref, weight_ref, residual_ref, new_ref, res_ref, next_ref, sems
):
    rotor = lax.axis_index("inst") < ROTOR_INST
    axial = cells_ref.shape[1]
    depth = packed_ref.shape[1] - ROWS
    per = axial // depth
    row = lax.broadcasted_iota(jnp.int32, (ROWS, LANES), 0)
    lower = row < 4

    def spread(ref, first, second):
        return jnp.where(
            lower,
            jnp.broadcast_to(ref[first : first + 1, :], (ROWS, LANES)),
            jnp.broadcast_to(ref[second : second + 1, :], (ROWS, LANES)),
        )

    inst0, inst2 = spread(inst_ref, 0, 1), spread(inst_ref, 2, 3)
    weight0, weight2 = spread(weight_ref, 0, 1), spread(weight_ref, 2, 3)
    total = jnp.zeros((ROWS, LANES), jnp.float32)
    for i in range(INST):
        coef = jnp.where(inst0 == i, weight0, 0.0) + jnp.where(inst2 == i, weight2, 0.0)
        total = total + coef * packed_ref[COLLECT.index(i), depth : depth + ROWS, :]
    ghost = total + pltpu.roll(total, 4, 0)
    ghost = [jnp.broadcast_to(ghost[c : c + 1, :], (ROWS, LANES)) for c in range(4)]
    flux_x, _ = fluxes(*ghost)
    head = jnp.logical_and(row == 0, jnp.logical_not(rotor))
    tail = jnp.logical_and(row == ROWS - 1, rotor)
    copies = []
    for c in range(4):
        half, damped = 0.5 * flux_x[c], DAMPING_COEF * ghost[c]
        at_head = jnp.where(head, -half - damped, 0.0)
        at_tail = jnp.where(tail, half - damped, 0.0)
        for j in range(per):

            def strip(t, carry, c=c, j=j):
                rows = pl.ds(pl.multiple_of(j * depth + t * ROWS, ROWS), ROWS)
                mine = pl.ds(pl.multiple_of(t * ROWS, ROWS), ROWS)
                out = partial_ref[c, rows, :] + packed_ref[COLLECT.index(SPREAD[c * per + j]), mine, :]
                res_ref[c, rows, :] = out
                next_ref[c, rows, :] = cells_ref[c, rows, :] - PSEUDO_STEP * out
                return carry

            lax.fori_loop(0, depth // ROWS, strip, 0, unroll=True)
        for first, extra in ((0, at_head), (axial - ROWS, at_tail)):
            out = res_ref[c, first : first + ROWS, :] + extra
            res_ref[c, first : first + ROWS, :] = out
            next_ref[c, first : first + ROWS, :] = cells_ref[c, first : first + ROWS, :] - PSEUDO_STEP * out
        for k, (src, dst) in enumerate(((res_ref, residual_ref), (next_ref, new_ref))):
            copy = pltpu.make_async_copy(src.at[c], dst.at[c], sems.at[2 * c + k])
            copy.start()
            copies.append(copy)
    for copy in copies:
        copy.wait()


def collected(block, axis):
    count = lax.axis_size(axis)
    for step in (1, count // 4):
        blocks = [block]
        for k in range(1, 4):
            pairs = [((i + k * step) % count, i) for i in range(count)]
            blocks.append(lax.ppermute(block, axis, pairs))
        block = jnp.concatenate(blocks, 0)
    return block


def on_device(state, src_inst, src_face, weights):
    cells = state[0]
    axial, width = cells.shape[1], cells.shape[2]
    inst_count = lax.axis_size("inst")
    cell_count = lax.axis_size("cell")
    depth = 4 * axial // inst_count

    vmem = pl.BlockSpec(memory_space=pltpu.VMEM)
    anywhere = pl.BlockSpec(memory_space=pl.ANY)
    sent = pl.pallas_call(
        send_kernel,
        out_shape=jax.ShapeDtypeStruct((inst_count, depth + ROWS, width), jnp.float32),
        in_specs=[anywhere, anywhere],
        out_specs=anywhere,
        scratch_shapes=[
            pltpu.VMEM((inst_count, depth + ROWS, width), jnp.float32),
            pltpu.VMEM(src_face.shape, jnp.int32),
            pltpu.SemaphoreType.DMA((1 + 2 * PIECES,)),
        ],
        compiler_params=pltpu.CompilerParams(vmem_limit_bytes=60 << 20),
        name="send",
    )(cells.reshape(inst_count, depth, width), src_face)
    sent, cells = lax.optimization_barrier((sent, cells))
    rotor = lax.axis_index("inst") < ROTOR_INST
    export = jnp.where(rotor, cells[:, -1, :], cells[:, 0, :])
    head, tail = pl.pallas_call(
        edge_kernel,
        out_shape=[
            jax.ShapeDtypeStruct((4, axial), jnp.float32),
            jax.ShapeDtypeStruct((4, axial), jnp.float32),
        ],
        in_specs=[vmem],
        out_specs=[vmem] * 2,
        compiler_params=pltpu.CompilerParams(vmem_limit_bytes=16 << 20),
        cost_estimate=pl.CostEstimate(flops=0, bytes_accessed=32 << 20, transcendentals=0),
        name="edges",
    )(cells)
    gathered = lax.all_to_all(sent, "inst", 0, 0, axis_index_groups=[SPREAD])
    faces = collected(export, "cell").reshape(cell_count, 4, width)
    faces = jnp.concatenate([faces, faces], 1).reshape(cell_count * ROWS, width)
    packed = pl.pallas_call(
        source_kernel,
        out_shape=jax.ShapeDtypeStruct((inst_count, depth + ROWS, width), jnp.float32),
        in_specs=[vmem, vmem],
        out_specs=anywhere,
        scratch_shapes=[
            pltpu.VMEM((inst_count, depth + ROWS, width), jnp.float32),
            pltpu.SemaphoreType.DMA((PIECES,)),
        ],
        compiler_params=pltpu.CompilerParams(vmem_limit_bytes=16 << 20),
        name="source",
    )(gathered, faces)
    head, tail, packed = lax.optimization_barrier((head, tail, packed))
    packed = lax.all_to_all(packed, "inst", 0, 0, axis_index_groups=[COLLECT])

    right = lax.ppermute(head, "cell", [((i + 1) % cell_count, i) for i in range(cell_count)])
    left = lax.ppermute(tail, "cell", [(i, (i + 1) % cell_count) for i in range(cell_count)])

    blocks = axial // depth
    per = depth // ROWS
    strips = axial // ROWS
    block_spec = pl.BlockSpec((4, depth, width), lambda g: (0, g, 0))
    halo_spec = pl.BlockSpec((4, depth), lambda g: (0, g))
    partial = pl.pallas_call(
        partial_kernel,
        grid=(blocks,),
        out_shape=pltpu.VMEM(cells.shape, jnp.float32),
        in_specs=[
            block_spec,
            pl.BlockSpec((4, ROWS, width), lambda g: (0, jnp.maximum(g * per - 1, 0), 0)),
            pl.BlockSpec((4, ROWS, width), lambda g: (0, jnp.minimum(g * per + per, strips - 1), 0)),
            halo_spec,
            halo_spec,
        ],
        out_specs=block_spec,
        scratch_shapes=[
            pltpu.VMEM((4, depth + 2 * ROWS, width), jnp.float32),
            pltpu.VMEM((4, depth + 2 * ROWS, width), jnp.float32),
            pltpu.VMEM((depth, width), jnp.float32),
        ],
        compiler_params=pltpu.CompilerParams(vmem_limit_bytes=16 << 20),
        cost_estimate=pl.CostEstimate(flops=100 * cells.size, bytes_accessed=16 * cells.size, transcendentals=0),
        name="partial",
    )(cells, cells, cells, right, left)
    residual, new_state = pl.pallas_call(
        finish_kernel,
        out_shape=[jax.ShapeDtypeStruct(cells.shape, jnp.float32)] * 2,
        in_specs=[vmem] * 5,
        out_specs=[anywhere, anywhere],
        scratch_shapes=[
            pltpu.VMEM(cells.shape, jnp.float32),
            pltpu.VMEM(cells.shape, jnp.float32),
            pltpu.SemaphoreType.DMA((8,)),
        ],
        compiler_params=pltpu.CompilerParams(vmem_limit_bytes=16 << 20),
        name="finish",
    )(packed, partial, cells, src_inst[:, 0, :], weights[:, 0, :])
    return residual[None], new_state[None]


def solution(mesh):
    return jax.shard_map(
        on_device,
        mesh=mesh,
        in_specs=(
            P("inst", None, None, "cell"),
            P(None, "inst", "cell"),
            P(None, "inst", "cell"),
            P(None, "inst", "cell"),
        ),
        out_specs=(P("inst", None, None, "cell"), P("inst", None, None, "cell")),
        check_vma=False,
    )
```

```python
import jax
import jax.numpy as jnp
import numpy as np
from jax import lax
from jax.experimental import pallas as pl
from jax.experimental.pallas import tpu as pltpu
from jax.sharding import PartitionSpec as P

ROTOR_INST = 9
STATOR_INST = 7
INST = ROTOR_INST + STATOR_INST
OMEGA_ROTOR = 0.8
OMEGA_STATOR = 0.6
GAMMA_LESS = 0.4
DAMPING_COEF = 0.05
PSEUDO_STEP = 0.2
LANES = 128
ROWS = 8
PIECES = 4
SPREAD = (8, 12, 3, 4, 6, 15, 10, 14, 13, 1, 9, 2, 5, 7, 0, 11)
COLLECT = (0, 4, 8, 12, 2, 6, 10, 14, 1, 5, 9, 13, 3, 7, 11, 15)


def pitch_coefficients(count, omega):
    steps = np.arange(1, (count - 1) // 2 + 1)
    return omega * 0.5 * np.power(-1.0, steps) / np.sin(np.pi * steps / count)


def coupled(values, omega):
    count = len(values)
    coefs = pitch_coefficients(count, omega)
    outs = []
    for i in range(count):
        total = None
        for d, coef in enumerate(coefs, 1):
            term = float(coef) * (values[(i - d) % count] - values[(i + d) % count])
            total = term if total is None else total + term
        outs.append(total)
    return outs


def send_kernel(cells_ref, face_ref, out_ref, held_ref, want_ref, sems):
    count, depth = out_ref.shape[0], out_ref.shape[1] - ROWS
    group = count // PIECES
    asked = pltpu.make_async_copy(face_ref, want_ref, sems.at[0])
    asked.start()
    arrivals = []
    for p in range(PIECES):
        part = pl.ds(p * group, group)
        copy = pltpu.make_async_copy(cells_ref.at[part], held_ref.at[part, pl.ds(0, depth), :], sems.at[1 + p])
        copy.start()
        arrivals.append(copy)
    asked.wait()
    lower = lax.broadcasted_iota(jnp.int32, (ROWS, LANES), 0) < 4
    want = jnp.where(
        lower,
        jnp.broadcast_to(want_ref[0], (ROWS, LANES)),
        jnp.broadcast_to(want_ref[1], (ROWS, LANES)),
    ).astype(jnp.float32)
    for j in range(count):
        held_ref[j, depth : depth + ROWS, :] = want
    leaving = []
    for p in range(PIECES):
        part = pl.ds(p * group, group)
        arrivals[p].wait()
        copy = pltpu.make_async_copy(held_ref.at[part], out_ref.at[part], sems.at[1 + PIECES + p])
        copy.start()
        leaving.append(copy)
    for copy in leaving:
        copy.wait()


def source_kernel(gathered_ref, faces_ref, out_ref, held_ref, sems):
    depth = gathered_ref.shape[1] - ROWS
    slab = lax.axis_index("cell")
    slabs = faces_ref.shape[0] // ROWS
    span = depth // PIECES
    leaving = []

    def leave(k, first, size):
        part = pl.ds(first, size)
        copy = pltpu.make_async_copy(held_ref.at[:, part, :], out_ref.at[:, part, :], sems.at[k])
        copy.start()
        leaving.append(copy)

    def tile(ahead):
        place = ahead
        return faces_ref[pl.ds(pl.multiple_of(place * ROWS, ROWS), ROWS), :]

    wants = [gathered_ref[i, depth : depth + ROWS, :].astype(jnp.int32) for i in range(INST)]
    firsts = [want[0, 0] >> 7 for want in wants]

    for p in range(PIECES):
        for t in range(p * span, (p + 1) * span, ROWS):
            values = [gathered_ref[SPREAD.index(i), t : t + ROWS, :] for i in range(INST)]
            outs = coupled(values[:ROTOR_INST], OMEGA_ROTOR) + coupled(values[ROTOR_INST:], OMEGA_STATOR)
            for i in range(INST):
                held_ref[COLLECT.index(i), t : t + ROWS, :] = outs[i]
        if p < PIECES - 1:
            leave(p, p * span, span)
    for i, (want, first) in enumerate(zip(wants, firsts)):
        ahead = (first - slab) & (slabs - 1)
        place = want & (LANES - 1)
        here = jnp.take_along_axis(tile(ahead), place, axis=1, mode="promise_in_bounds")
        after = jnp.take_along_axis(tile((ahead + 1) & (slabs - 1)), place, axis=1, mode="promise_in_bounds")
        held_ref[COLLECT.index(SPREAD[i]), depth : depth + ROWS, :] = jnp.where((want >> 7) == first, here, after)
    leave(PIECES - 1, depth - span, span + ROWS)
    for copy in leaving:
        copy.wait()


def fluxes(r, m, n, e):
    inv = 1.0 / r
    a = m * inv
    b = n * inv
    ma = m * a
    mb = m * b
    nb = n * b
    p = GAMMA_LESS * (e - 0.5 * (ma + nb))
    h = e + p
    return (m, ma + p, mb, h * a), (n, mb, nb + p, h * b)


def edge_kernel(cells_ref, head_ref, tail_ref):
    axial = cells_ref.shape[1]
    lane = lax.broadcasted_iota(jnp.int32, (LANES, LANES), 1)
    for first in range(0, axial, LANES):
        span = pl.ds(first, LANES)
        sides = jnp.zeros((LANES, LANES), jnp.float32)
        for c in range(4):
            u = cells_ref[c, span, :]
            sides = jnp.where(lane == c, pltpu.roll(u, c, 1) if c else u, sides)
            sides = jnp.where(lane == 4 + c, pltpu.roll(u, 5 + c, 1), sides)
        sides = sides.T
        for ref, at, sign in ((head_ref, 0, -1.0), (tail_ref, 4, 1.0)):
            u = [sides[at + c : at + c + 1, :] for c in range(4)]
            _, flux_y = fluxes(*u)
            for c in range(4):
                ref[c : c + 1, span] = 0.5 * flux_y[c] + sign * DAMPING_COEF * u[c]


def partial_kernel(
    cur_ref, prev_ref, next_ref, right_ref, left_ref, out_ref, plus_ref, minus_ref, side_ref
):
    block = pl.program_id(0)
    last = pl.num_programs(0) - 1
    size = cur_ref.shape[1]
    rotor = lax.axis_index("inst") < ROTOR_INST

    def edge(outer, own, at_end):
        return [jnp.where(at_end, jnp.broadcast_to(own[c], (ROWS, LANES)), outer[c]) for c in range(4)]

    before = edge([prev_ref[c] for c in range(4)], [cur_ref[c, 0:1, :] for c in range(4)], block == 0)
    after = edge(
        [next_ref[c] for c in range(4)], [cur_ref[c, size - 1 : size, :] for c in range(4)], block == last
    )
    keep_before = jnp.where(jnp.logical_or(block > 0, rotor), 1.0, 0.0)
    keep_after = jnp.where(jnp.logical_and(block == last, rotor), 0.0, 1.0)
    flux_before, _ = fluxes(*before)
    flux_after, _ = fluxes(*after)
    for c in range(4):
        minus_ref[c, 0:ROWS, :] = keep_before * (0.5 * flux_before[c] + DAMPING_COEF * before[c])
        plus_ref[c, size + ROWS : size + 2 * ROWS, :] = keep_after * (
            0.5 * flux_after[c] - DAMPING_COEF * after[c]
        )

    lane = lax.broadcasted_iota(jnp.int32, (ROWS, LANES), 1)
    sides = jnp.concatenate([right_ref[...], left_ref[...], jnp.zeros((LANES - 8, LANES), jnp.float32)], 0)
    side_ref[...] = sides.T

    def first(t, carry):
        rows = pl.ds(pl.multiple_of(t * ROWS, ROWS), ROWS)
        shifted = pl.ds(pl.multiple_of(t * ROWS + ROWS, ROWS), ROWS)
        u = [cur_ref[c, rows, :] for c in range(4)]
        flux_x, flux_y = fluxes(*u)
        side = side_ref[rows, :]
        for c in range(4):
            half_x = 0.5 * flux_x[c]
            half_y = 0.5 * flux_y[c]
            damped = DAMPING_COEF * u[c]
            plus_ref[c, shifted, :] = half_x - damped
            minus_ref[c, shifted, :] = half_x + damped
            up = jnp.where(lane == 0, jnp.broadcast_to(side[:, c : c + 1], (ROWS, LANES)), half_y - damped)
            down = jnp.where(lane == LANES - 1, jnp.broadcast_to(side[:, 4 + c : 5 + c], (ROWS, LANES)), half_y + damped)
            out_ref[c, rows, :] = (
                pltpu.roll(up, LANES - 1, 1) - pltpu.roll(down, 1, 1) + (4.0 * DAMPING_COEF) * u[c]
            )
        return carry

    lax.fori_loop(0, size // ROWS, first, 0, unroll=4)

    for t in range(size // ROWS):
        lo = t * ROWS
        for c in range(4):
            out_ref[c, lo : lo + ROWS, :] = (
                out_ref[c, lo : lo + ROWS, :]
                + plus_ref[c, lo + ROWS + 1 : lo + 2 * ROWS + 1, :]
                - minus_ref[c, lo + ROWS - 1 : lo + 2 * ROWS - 1, :]
            )


def finish_kernel(
    packed_ref, partial_ref, cells_ref, inst_ref, weight_ref, residual_ref, new_ref, res_ref, next_ref, sems
):
    rotor = lax.axis_index("inst") < ROTOR_INST
    axial = cells_ref.shape[1]
    depth = packed_ref.shape[1] - ROWS
    per = axial // depth
    row = lax.broadcasted_iota(jnp.int32, (ROWS, LANES), 0)
    lower = row < 4

    def spread(ref, first, second):
        return jnp.where(
            lower,
            jnp.broadcast_to(ref[first : first + 1, :], (ROWS, LANES)),
            jnp.broadcast_to(ref[second : second + 1, :], (ROWS, LANES)),
        )

    inst0, inst2 = spread(inst_ref, 0, 1), spread(inst_ref, 2, 3)
    weight0, weight2 = spread(weight_ref, 0, 1), spread(weight_ref, 2, 3)
    total = jnp.zeros((ROWS, LANES), jnp.float32)
    for i in range(INST):
        coef = jnp.where(inst0 == i, weight0, 0.0) + jnp.where(inst2 == i, weight2, 0.0)
        total = total + coef * packed_ref[COLLECT.index(i), depth : depth + ROWS, :]
    ghost = total + pltpu.roll(total, 4, 0)
    ghost = [jnp.broadcast_to(ghost[c : c + 1, :], (ROWS, LANES)) for c in range(4)]
    flux_x, _ = fluxes(*ghost)
    head = jnp.logical_and(row == 0, jnp.logical_not(rotor))
    tail = jnp.logical_and(row == ROWS - 1, rotor)
    copies = []
    for c in range(4):
        half, damped = 0.5 * flux_x[c], DAMPING_COEF * ghost[c]
        at_head = jnp.where(head, -half - damped, 0.0)
        at_tail = jnp.where(tail, half - damped, 0.0)
        for j in range(per):

            def strip(t, carry, c=c, j=j):
                rows = pl.ds(pl.multiple_of(j * depth + t * ROWS, ROWS), ROWS)
                mine = pl.ds(pl.multiple_of(t * ROWS, ROWS), ROWS)
                out = partial_ref[c, rows, :] + packed_ref[COLLECT.index(SPREAD[c * per + j]), mine, :]
                res_ref[c, rows, :] = out
                next_ref[c, rows, :] = cells_ref[c, rows, :] - PSEUDO_STEP * out
                return carry

            lax.fori_loop(0, depth // ROWS, strip, 0, unroll=True)
            if 0 < j < per - 1:
                for k, (src, dst) in enumerate(((res_ref, residual_ref), (next_ref, new_ref))):
                    span = pl.ds(j * depth, depth)
                    copy = pltpu.make_async_copy(
                        src.at[c, span, :], dst.at[c, span, :], sems.at[2 * (c * per + j) + k]
                    )
                    copy.start()
                    copies.append(copy)
        for first, extra in ((0, at_head), (axial - ROWS, at_tail)):
            out = res_ref[c, first : first + ROWS, :] + extra
            res_ref[c, first : first + ROWS, :] = out
            next_ref[c, first : first + ROWS, :] = cells_ref[c, first : first + ROWS, :] - PSEUDO_STEP * out
        for j in (0, per - 1):
            for k, (src, dst) in enumerate(((res_ref, residual_ref), (next_ref, new_ref))):
                span = pl.ds(j * depth, depth)
                copy = pltpu.make_async_copy(
                    src.at[c, span, :], dst.at[c, span, :], sems.at[2 * (c * per + j) + k]
                )
                copy.start()
                copies.append(copy)
    for copy in copies:
        copy.wait()


def collected(block, axis):
    count = lax.axis_size(axis)
    for step in (1, count // 4):
        blocks = [block]
        for k in range(1, 4):
            pairs = [((i + k * step) % count, i) for i in range(count)]
            blocks.append(lax.ppermute(block, axis, pairs))
        block = jnp.concatenate(blocks, 0)
    return block


def on_device(state, src_inst, src_face, weights):
    cells = state[0]
    axial, width = cells.shape[1], cells.shape[2]
    inst_count = lax.axis_size("inst")
    cell_count = lax.axis_size("cell")
    depth = 4 * axial // inst_count

    vmem = pl.BlockSpec(memory_space=pltpu.VMEM)
    anywhere = pl.BlockSpec(memory_space=pl.ANY)
    sent = pl.pallas_call(
        send_kernel,
        out_shape=jax.ShapeDtypeStruct((inst_count, depth + ROWS, width), jnp.float32),
        in_specs=[anywhere, anywhere],
        out_specs=anywhere,
        scratch_shapes=[
            pltpu.VMEM((inst_count, depth + ROWS, width), jnp.float32),
            pltpu.VMEM(src_face.shape, jnp.int32),
            pltpu.SemaphoreType.DMA((1 + 2 * PIECES,)),
        ],
        compiler_params=pltpu.CompilerParams(vmem_limit_bytes=60 << 20),
        name="send",
    )(cells.reshape(inst_count, depth, width), src_face)
    sent, cells = lax.optimization_barrier((sent, cells))
    rotor = lax.axis_index("inst") < ROTOR_INST
    export = jnp.where(rotor, cells[:, -1, :], cells[:, 0, :])
    head, tail = pl.pallas_call(
        edge_kernel,
        out_shape=[
            jax.ShapeDtypeStruct((4, axial), jnp.float32),
            jax.ShapeDtypeStruct((4, axial), jnp.float32),
        ],
        in_specs=[vmem],
        out_specs=[vmem] * 2,
        compiler_params=pltpu.CompilerParams(vmem_limit_bytes=16 << 20),
        cost_estimate=pl.CostEstimate(flops=0, bytes_accessed=32 << 20, transcendentals=0),
        name="edges",
    )(cells)
    gathered = lax.all_to_all(sent, "inst", 0, 0, axis_index_groups=[SPREAD])
    faces = collected(export, "cell").reshape(cell_count, 4, width)
    faces = jnp.concatenate([faces, faces], 1).reshape(cell_count * ROWS, width)
    packed = pl.pallas_call(
        source_kernel,
        out_shape=jax.ShapeDtypeStruct((inst_count, depth + ROWS, width), jnp.float32),
        in_specs=[vmem, vmem],
        out_specs=anywhere,
        scratch_shapes=[
            pltpu.VMEM((inst_count, depth + ROWS, width), jnp.float32),
            pltpu.SemaphoreType.DMA((PIECES,)),
        ],
        compiler_params=pltpu.CompilerParams(vmem_limit_bytes=16 << 20),
        name="source",
    )(gathered, faces)
    head, tail, packed = lax.optimization_barrier((head, tail, packed))
    packed = lax.all_to_all(packed, "inst", 0, 0, axis_index_groups=[COLLECT])

    right = lax.ppermute(head, "cell", [((i + 1) % cell_count, i) for i in range(cell_count)])
    left = lax.ppermute(tail, "cell", [(i, (i + 1) % cell_count) for i in range(cell_count)])

    blocks = axial // depth
    per = depth // ROWS
    strips = axial // ROWS
    block_spec = pl.BlockSpec((4, depth, width), lambda g: (0, g, 0))
    halo_spec = pl.BlockSpec((4, depth), lambda g: (0, g))
    partial = pl.pallas_call(
        partial_kernel,
        grid=(blocks,),
        out_shape=pltpu.VMEM(cells.shape, jnp.float32),
        in_specs=[
            block_spec,
            pl.BlockSpec((4, ROWS, width), lambda g: (0, jnp.maximum(g * per - 1, 0), 0)),
            pl.BlockSpec((4, ROWS, width), lambda g: (0, jnp.minimum(g * per + per, strips - 1), 0)),
            halo_spec,
            halo_spec,
        ],
        out_specs=block_spec,
        scratch_shapes=[
            pltpu.VMEM((4, depth + 2 * ROWS, width), jnp.float32),
            pltpu.VMEM((4, depth + 2 * ROWS, width), jnp.float32),
            pltpu.VMEM((depth, width), jnp.float32),
        ],
        compiler_params=pltpu.CompilerParams(vmem_limit_bytes=16 << 20),
        cost_estimate=pl.CostEstimate(flops=100 * cells.size, bytes_accessed=16 * cells.size, transcendentals=0),
        name="partial",
    )(cells, cells, cells, right, left)
    residual, new_state = pl.pallas_call(
        finish_kernel,
        out_shape=[jax.ShapeDtypeStruct(cells.shape, jnp.float32)] * 2,
        in_specs=[vmem] * 5,
        out_specs=[anywhere, anywhere],
        scratch_shapes=[
            pltpu.VMEM(cells.shape, jnp.float32),
            pltpu.VMEM(cells.shape, jnp.float32),
            pltpu.SemaphoreType.DMA((2 * inst_count,)),
        ],
        compiler_params=pltpu.CompilerParams(vmem_limit_bytes=16 << 20),
        name="finish",
    )(packed, partial, cells, src_inst[:, 0, :], weights[:, 0, :])
    return residual[None], new_state[None]


def solution(mesh):
    return jax.shard_map(
        on_device,
        mesh=mesh,
        in_specs=(
            P("inst", None, None, "cell"),
            P(None, "inst", "cell"),
            P(None, "inst", "cell"),
            P(None, "inst", "cell"),
        ),
        out_specs=(P("inst", None, None, "cell"), P("inst", None, None, "cell")),
        check_vma=False,
    )
```
